32 devices in a mesh: seq: 8 (over y, x, core), expert: 4 (over z).
Axes of the slice: x: 2, y: 2, z: 4, core: 2. Of those that a mesh axis runs over, the one named last changes fastest.
Arguments:
- layer_input: bfloat16 [512, 2, 4096], P(('seq', 'expert')), may hold values from -6 to 6
- x_branch: bfloat16 [512, 2, 4096], P('seq', None, 'expert'), may hold values from -24 to 24
- gate_branch: bfloat16 [512, 2, 4096], P('seq', None, 'expert'), may hold values from -6 to 6
- conv_weight: bfloat16 [4, 4096], P(None, 'expert'), may hold values from -3 to 3
- conv_bias: bfloat16 [4096], P('expert'), may hold values from -3 to 3
- x_proj: bfloat16 [4096, 288], P('expert'), may hold values from -0.09375 to 0.09375
- dt_proj: bfloat16 [256, 4096], P(None, 'expert'), may hold values from -0.375 to 0.375
- dt_bias: float32 [4096], P('expert'), may hold values from -5.5 to -2
- a_log: float32 [4096, 16], P('expert'), may hold values from -7 to 2.77
- d_skip: float32 [4096], P('expert'), may hold values from 0.5 to 1.5
- carry_state: float32 [2, 4096, 16], P(None, 'expert'), may hold values from -3 to 3
- carry_tail: bfloat16 [3, 2, 4096], P(None, None, 'expert'), may hold values from -6 to 6
- out_proj: bfloat16 [4096, 4096], P('expert'), may hold values from -0.09375 to 0.09375
- steering: bfloat16 [4096], replicated, may hold values from -6 to 6
- refusal: bfloat16 [4, 4096], replicated, may hold values from -6 to 6
- norm_gain: bfloat16 [4096], replicated, may hold values from 0.5 to 1.5
- router: bfloat16 [4096, 4], replicated, may hold values from -0.09375 to 0.09375
- specialist_switch_matrix: bfloat16 [4, 4096, 2048], P('expert', None, 'seq'), may hold values from -0.09375 to 0.09375
- w_up: bfloat16 [4, 4096, 2048], P('expert', None, 'seq'), may hold values from -0.09375 to 0.09375
- w_down: bfloat16 [4, 2048, 4096], P('expert', 'seq'), may hold values from -0.125 to 0.125
- expert_ids: int32 [512, 2, 2], P('seq'), may hold values from 0 to 3, all different within a row; in each aligned block of 128 rows (0 to 127, 128 to 255, ..., all dimensions but the last counted through in order) at most 80 rows name the same one
Outputs:
- layer_out: float32 [512, 2, 4096], P(('seq', 'expert'))
The draws below stay inside these ranges and needn't reach their ends.
Inputs may be any that keep to these rules, and one draw needn't show every extreme that they name: `expert_ids`: in every aligned block of 128 rows in position-major order (the tokens of one seq index), no expert is named by more than 80 tokens, and in some block an expert is named by exactly 80; the two experts of a token differ.
All inputs are finite; a program needn't handle non-finite values.
Results may differ from the reference program's by a relative error of at most 0.0044.
Values may be sent and summed in bfloat16 or wider, within the bound.
A program may use at most 128 MiB of HBM per device.

```python
import math
import jax
import jax.numpy as jnp
import numpy as np
from jax import lax

D = 4096
ECH = 4096
NST = 16
KCONV = 4
RANK = 256
DIRS = 4
TOP = 2
FF_DEV = 256
PROMPTS = 2
TOK_SEQ = 64
EXPERTS = 4
FF = 2048
LEN = 512
MOST = 80
N_SEQ = 8


def draw_x_branch(key, part):
    base_key, selection_key = jax.random.split(jax.random.fold_in(key, 11))
    specialist_choices = jax.random.randint(selection_key, (6,), 0, LEN)
    word_locations = jnp.arange(LEN)
    word_group_run = jnp.any(word_locations[:, None] == specialist_choices[None, :], axis=1)
    multiplier_value = jnp.where(word_group_run, 4.0, 1.0).astype(jnp.float32)
    base = jnp.clip(jax.random.normal(base_key, (LEN, PROMPTS, ECH), jnp.float32), -6.0, 6.0)
    return (base * multiplier_value[:, None, None]).astype(jnp.bfloat16)


def draw_dt_bias(key, part):
    uniform_draw = jax.random.uniform(jax.random.fold_in(key, 23), (ECH,), jnp.float32)
    lower, upper = (0.01, 0.1)
    initial = jnp.exp(jnp.log(lower) + uniform_draw * (jnp.log(upper) - jnp.log(lower)))
    return (initial + jnp.log(-jnp.expm1(-initial))).astype(jnp.float32)


def levels(own_key, dims, cuts, smallest, top_value):
    gain, own = 1.0, jax.random.fold_in(own_key, 6)
    for dim, blocks in cuts:
        draws = jnp.exp(jax.random.uniform(jax.random.fold_in(own, dim), (blocks,), jnp.float32, smallest / len(cuts), top_value / len(cuts)))
        gain = gain * jnp.repeat(draws, dims[dim] // blocks).reshape([-1 if axis == dim else 1 for axis in range(len(dims))])
    return gain


def assign_block(stream_key, own, number, rows, count, top, reach, slope):
    ranking = jax.random.permutation(stream_key, count)
    heavy_load, common = load_shares(count, rows * top, reach, slope, True), load_shares(count, rows * top, reach, slope, False)
    places = jnp.arange(count)

    def named(sizes, turn):
        used = int((sizes > 0).sum())
        fixed = max(1, used // 4)
        shifted = fixed + (places - fixed + turn * (used - fixed)) % max(1, count - fixed)
        return jnp.zeros((count,), jnp.int32).at[ranking[jnp.where(places < fixed, places, shifted)]].set(jnp.asarray(sizes, jnp.int32))

    sizes = jnp.where(number % 4 == 0, named(heavy_load, number // 4), named(common, number - number // 4 - 1))
    mixed = jax.random.permutation(jax.random.fold_in(own, 3), count)
    giver, taker = mixed[0:count // 2 * 2:2], mixed[1:count // 2 * 2:2]
    margin = jnp.minimum(sizes[giver] - 1, reach - sizes[taker]) // 2
    margin = jnp.where((giver == ranking[0]) | (taker == ranking[0]) | (sizes[taker] == 0), 0, jnp.maximum(margin, 0))
    shifted = jax.random.randint(jax.random.fold_in(own, 4), (count // 2,), 0, 1 << 20) % (margin + 1)
    sizes = sizes.at[giver].add(-shifted).at[taker].add(shifted)
    labels = jnp.searchsorted(jnp.cumsum(sizes), jnp.arange(rows * top), side="right").astype(jnp.int32)
    grid = labels.reshape(top, rows).T
    grid = grid[jax.random.permutation(jax.random.fold_in(own, 1), rows)]
    turn = jax.random.randint(jax.random.fold_in(own, 2), (rows, 1), 0, top)
    return jnp.take_along_axis(grid, (jnp.arange(top)[None, :] + turn) % top, axis=1)


def load_shares(count, total, bound, skew, full):
    portions = [(1 << 20) // math.isqrt(grade ** skew) + 1 for grade in range(1, count + 1)]
    largest = bound if full else min(bound, max(-(-total // count), total * portions[0] // sum(portions)))
    least = 1 if total - largest >= count - 1 else 0
    counts, surplus = [largest] + [least] * (count - 1), total - largest - least * (count - 1)
    while surplus > 0:
        candidates = [i for i in range(1, count) if counts[i] < largest] or [i for i in range(1, count) if counts[i] < bound]
        pool, budget = sum([portions[i] for i in candidates]), surplus
        for i in candidates:
            more = min(bound - counts[i], max(1, budget * portions[i] // pool), surplus)
            counts[i] = counts[i] + more
            surplus = surplus - more
    return np.array(counts)


def scatter_about(key, dims, spread, most, cuts=(), held_as=jnp.bfloat16):
    drawn = jax.random.normal(key, dims, jnp.float32) * spread
    if len(cuts) > 0:
        drawn = levels(key, dims, cuts, -0.22, 0.18) * drawn
    return jnp.clip(drawn, min=-most, max=most).astype(held_as)


def setup_inputs(seed: int = 0) -> dict:
    key_list = jax.random.split(jax.random.key(seed), 22)
    layer_input = scatter_about(key_list[0], (LEN, PROMPTS, D), 1.0, 6.0, ((0, 32),))
    x_branch = draw_x_branch(jax.random.fold_in(key_list[21], 71), 0)
    gate_branch = scatter_about(key_list[2], (LEN, PROMPTS, ECH), 1.0, 6.0, ((0, 8), (2, 4)))
    conv_weight = scatter_about(key_list[3], (KCONV, ECH), KCONV ** -0.5, 3.0, ((1, 4),))
    conv_bias = scatter_about(key_list[4], (ECH,), 0.5, 3.0, ((0, 4),))
    x_proj = scatter_about(key_list[5], (ECH, RANK + 2 * NST), ECH ** -0.5, 0.09375, ((0, 4),))
    dt_proj = scatter_about(key_list[6], (RANK, ECH), RANK ** -0.5, 0.375, ((1, 4),))
    dt_bias = draw_dt_bias(jax.random.fold_in(key_list[21], 71), 0)
    a_log = jnp.clip(-7.0 + 9.77 * jax.random.uniform(key_list[8], (ECH, NST), jnp.float32) ** levels(key_list[8], (ECH, NST), ((0, 4),), -0.2, 0.2), -7.0, 2.77)
    d_skip = jnp.clip(0.5 + 1.0 * jax.random.uniform(key_list[9], (ECH,), jnp.float32) ** levels(key_list[9], (ECH,), ((0, 4),), -0.2, 0.2), 0.5, 1.5)
    carry_state = scatter_about(key_list[10], (PROMPTS, ECH, NST), 0.5, 3.0, ((1, 4),), jnp.float32)
    carry_tail = scatter_about(key_list[11], (KCONV - 1, PROMPTS, ECH), 1.0, 6.0, ((2, 4),))
    out_proj = scatter_about(key_list[12], (ECH, D), ECH ** -0.5, 0.09375, ((0, 4),))
    steering = scatter_about(key_list[13], (D,), 1.0, 6.0)
    refusal = scatter_about(key_list[14], (DIRS, D), 1.0, 6.0)
    norm_gain = jnp.clip(1.0 + 0.1 * jax.random.normal(key_list[15], (D,), jnp.float32), 0.5, 1.5).astype(jnp.bfloat16)
    router = scatter_about(key_list[16], (D, EXPERTS), D ** -0.5, 0.09375)
    specialist_switch_matrix = scatter_about(key_list[17], (EXPERTS, D, FF), D ** -0.5, 0.09375, ((0, 4), (2, 8)))
    w_up = scatter_about(key_list[18], (EXPERTS, D, FF), D ** -0.5, 0.09375, ((0, 4), (2, 8)))
    w_down = scatter_about(key_list[19], (EXPERTS, FF, D), FF ** -0.5, 0.125, ((0, 4), (1, 8)))
    expert_ids_keys = jax.random.split(jax.random.fold_in(key_list[20], 1), LEN * PROMPTS // (TOK_SEQ * PROMPTS))
    expert_ids_turns = jax.random.permutation(jax.random.fold_in(key_list[20], 3), LEN * PROMPTS // (TOK_SEQ * PROMPTS))
    expert_ids = jax.vmap(lambda own, number: assign_block(jax.random.fold_in(key_list[20], 2), own, number, TOK_SEQ * PROMPTS, EXPERTS, TOP, MOST, 1))(expert_ids_keys, expert_ids_turns).reshape((LEN, PROMPTS, TOP))
    return dict(layer_input=layer_input, x_branch=x_branch, gate_branch=gate_branch, conv_weight=conv_weight, conv_bias=conv_bias, x_proj=x_proj, dt_proj=dt_proj, dt_bias=dt_bias, a_log=a_log, d_skip=d_skip, carry_state=carry_state, carry_tail=carry_tail, out_proj=out_proj, steering=steering, refusal=refusal, norm_gain=norm_gain, router=router, specialist_switch_matrix=specialist_switch_matrix, w_up=w_up, w_down=w_down, expert_ids=expert_ids)


EPS = 1e-06

def remove_directions(steering, refusal):
    vector = steering.astype(jnp.float32)
    units = []
    for k in range(DIRS):
        r = refusal[k].astype(jnp.float32)
        for q in units:
            r = r - jnp.sum(q * r) * q
        r = r * lax.rsqrt(jnp.sum(r * r) + EPS)
        units.append(r)
    for q in units:
        vector = vector - jnp.sum(q * vector) * q
    return vector

def route_weights(normed, router, picked_indices):
    logits = jnp.dot(normed, router, preferred_element_type=jnp.float32)
    onehot = (picked_indices[:, :, None] == jnp.arange(EXPERTS, dtype=jnp.int32)[None, None, :]).astype(jnp.float32)
    picked = lax.optimization_barrier(jnp.sum(onehot * logits[:, None, :], axis=-1))
    leading = jax.nn.sigmoid(picked[:, 0] - picked[:, 1])
    shares = jnp.stack([leading, 1.0 - leading], axis=1)
    return lax.optimization_barrier(jnp.sum(onehot * shares[:, :, None], axis=1))

def reference(layer_input, x_branch, gate_branch, conv_weight, conv_bias, x_proj, dt_proj, dt_bias, a_log, d_skip, carry_state, carry_tail, out_proj, steering, refusal, norm_gain, router, specialist_switch_matrix, w_up, w_down, expert_ids):
    padded = jnp.concatenate([carry_tail, x_branch], axis=0).astype(jnp.float32)
    convolved = conv_bias.astype(jnp.float32)
    for k in range(KCONV):
        convolved = convolved + conv_weight[k].astype(jnp.float32) * padded[k:k + LEN]
    activated = jax.nn.silu(convolved)
    row_count = LEN * PROMPTS
    projected = jnp.dot(activated.astype(jnp.bfloat16).reshape(row_count, ECH), x_proj, preferred_element_type=jnp.float32)
    low = projected[:, :RANK].astype(jnp.bfloat16)
    input_matrix_b = projected[:, RANK:RANK + NST].reshape(LEN, PROMPTS, NST)
    c_output = projected[:, RANK + NST:].reshape(LEN, PROMPTS, NST)
    step_size = jax.nn.softplus(jnp.dot(low, dt_proj, preferred_element_type=jnp.float32) + dt_bias).reshape(LEN, PROMPTS, ECH)
    rate = -jnp.exp(a_log)

    def advance(carried, inputs):
        current_increment, act_now, b_now, c_now = inputs
        decays = jnp.exp(current_increment[:, :, None] * rate[None])
        carried = decays * carried + (current_increment * act_now)[:, :, None] * b_now[:, None, :]
        return (carried, lax.optimization_barrier(jnp.sum(carried * c_now[:, None, :], axis=-1)))
    _, scanned = lax.scan(advance, carry_state, (step_size, activated, input_matrix_b, c_output))
    output_y = scanned + d_skip * activated
    gated = (output_y * jax.nn.silu(gate_branch.astype(jnp.float32))).astype(jnp.bfloat16)
    mixed = jnp.dot(gated.reshape(row_count, ECH), out_proj, preferred_element_type=jnp.float32)
    steering_clean = remove_directions(steering, refusal)
    residual = layer_input.astype(jnp.float32).reshape(row_count, D) + mixed + steering_clean
    normed = (residual * lax.rsqrt(lax.optimization_barrier(jnp.mean(residual * residual, axis=-1, keepdims=True)) + EPS) * norm_gain.astype(jnp.float32)).astype(jnp.bfloat16)
    row_ids = expert_ids.reshape(row_count, TOP)
    weights = route_weights(normed, router, row_ids)
    capacity = N_SEQ * MOST

    def per_expert(total, items):
        expert_slot, gate_w, up_w, down_w = items
        member = jnp.any(row_ids == expert_slot, axis=1)
        count = jnp.sum(member.astype(jnp.int32))
        slot_index = jnp.nonzero(member, size=capacity, fill_value=0)[0].astype(jnp.int32)
        valid = (jnp.arange(capacity, dtype=jnp.int32) < count).astype(jnp.float32)
        inputs = normed[slot_index]
        gate = jnp.dot(inputs, gate_w, preferred_element_type=jnp.float32)
        upward = jnp.dot(inputs, up_w, preferred_element_type=jnp.float32)
        hidden = (jax.nn.silu(gate) * upward).astype(jnp.bfloat16)
        shards = hidden.reshape(capacity, N_SEQ, FF_DEV).transpose(1, 0, 2)
        downs = down_w.reshape(N_SEQ, FF_DEV, D)

        def add_shard(accum, pair):
            partial_out = jnp.dot(pair[0], pair[1], preferred_element_type=jnp.float32).astype(jnp.bfloat16)
            partial_out = lax.optimization_barrier(partial_out)
            return (accum + partial_out.astype(jnp.float32), None)
        expert_out, _ = lax.scan(add_shard, jnp.zeros((capacity, D), jnp.float32), (shards, downs))
        column = (jnp.arange(EXPERTS, dtype=jnp.int32) == expert_slot).astype(jnp.float32)
        share = lax.optimization_barrier(jnp.sum(weights[slot_index] * column[None, :], axis=1)) * valid
        total = total.at[slot_index].add(expert_out * share[:, None])
        return (total, None)
    moe_total, _ = lax.scan(per_expert, jnp.zeros((row_count, D), jnp.float32), (jnp.arange(EXPERTS, dtype=jnp.int32), specialist_switch_matrix, w_up, w_down))
    return (residual + moe_total).reshape(LEN, PROMPTS, D)
```

```python
import jax
import jax.numpy as jnp
from jax import lax
from jax.experimental import pallas as pl
from jax.experimental.pallas import tpu as pltpu
from jax.sharding import PartitionSpec as P

EPS = 1e-06
VMEM_LIMIT = 48 * 1024 * 1024
LANES = 128


def passed_along(array, axis, by):
    count = lax.axis_size(axis)
    pairs = [(i, i + by) for i in range(count) if 0 <= i + by < count]
    return lax.ppermute(array, axis, pairs)


def remove_directions(steering, refusal):
    vector = steering.astype(jnp.float32)
    units = []
    for k in range(refusal.shape[0]):
        r = refusal[k].astype(jnp.float32)
        for q in units:
            r = r - jnp.sum(q * r) * q
        r = r * lax.rsqrt(jnp.sum(r * r) + EPS)
        units.append(r)
    for q in units:
        vector = vector - jnp.sum(q * vector) * q
    return vector


def root_mean_normed(residual, norm_gain):
    scaled = residual * lax.rsqrt(jnp.mean(residual * residual, axis=-1, keepdims=True) + EPS)
    return (scaled * norm_gain.astype(jnp.float32)).astype(jnp.bfloat16)


def owner_weight(normed, router, picked_indices, owner):
    experts = router.shape[1]
    logits = jnp.dot(normed, router, preferred_element_type=jnp.float32)
    labels = jnp.arange(experts, dtype=jnp.int32)
    onehot = (picked_indices[:, :, None] == labels[None, None, :]).astype(jnp.float32)
    picked = jnp.sum(onehot * logits[:, None, :], axis=-1)
    leading = jax.nn.sigmoid(picked[:, 0] - picked[:, 1])
    shares = jnp.stack([leading, 1.0 - leading], axis=1)
    per_expert = jnp.sum(onehot * shares[:, :, None], axis=1)
    return jnp.sum(per_expert * (labels == owner).astype(jnp.float32)[None, :], axis=1)


def slot_matrix(picked_indices, owner, capacity):
    member = jnp.any(picked_indices == owner, axis=1)
    order = jnp.cumsum(member.astype(jnp.int32)) - 1
    slots = jnp.arange(capacity, dtype=jnp.int32)
    return (order[None, :] == slots[:, None]) & member[None, :]


def state_kernel(length, prompts, nst, groups, low_ref, dtp_ref, dtb_ref, act_ref, alog_ref, b_ref,
                 dtx_ref, actx_ref, state_ref, total_ref):
    rows = length * prompts
    for k in range(groups):
        cols = pl.ds(k * LANES, LANES)
        raw = jnp.dot(low_ref[...], dtp_ref[:, cols], preferred_element_type=jnp.float32)
        dtx_ref[pl.ds(k, rows, stride=groups), :] = jax.nn.softplus(raw + dtb_ref[:, cols])
        actx_ref[pl.ds(k, rows, stride=groups), :] = act_ref[:, cols]
    rates = [-jnp.exp(alog_ref[n]) for n in range(nst)]
    for p in range(prompts):

        def step(t, carry):
            states, total = carry
            row = t * prompts + p
            at = pl.ds(pl.multiple_of(row * groups, groups), groups)
            dt = dtx_ref[at, :]
            drive = dt * actx_ref[at, :]
            states = tuple(
                jnp.exp(dt * rates[n]) * states[n] + drive * b_ref[row * 2 * nst + n]
                for n in range(nst)
            )
            return states, total + dt

        zero = jnp.zeros((groups, LANES), jnp.float32)
        states, total = lax.fori_loop(0, length, step, ((zero,) * nst, zero), unroll=4)
        for n in range(nst):
            state_ref[p, n] = states[n]
        total_ref[p] = total


def output_kernel(length, prompts, nst, groups, dtx_ref, actx_ref, alog_ref, b_ref, enter_ref, skip_ref,
                  gate_ref, out_ref, y_ref):
    rows = length * prompts
    rates = [-jnp.exp(alog_ref[n]) for n in range(nst)]
    skip = skip_ref[...]
    for p in range(prompts):

        def step(t, states):
            row = t * prompts + p
            at = pl.ds(pl.multiple_of(row * groups, groups), groups)
            dt = dtx_ref[at, :]
            act = actx_ref[at, :]
            drive = dt * act
            y = skip * act
            fresh = []
            for n in range(nst):
                s = jnp.exp(dt * rates[n]) * states[n] + drive * b_ref[row * 2 * nst + n]
                y = y + s * b_ref[row * 2 * nst + nst + n]
                fresh.append(s)
            y_ref[at, :] = y
            return tuple(fresh)

        lax.fori_loop(0, length, step, tuple(enter_ref[p, n] for n in range(nst)), unroll=4)
    for k in range(groups):
        cols = pl.ds(k * LANES, LANES)
        gate = gate_ref[:, cols].astype(jnp.float32)
        y = y_ref[pl.ds(k, rows, stride=groups), :]
        out_ref[:, cols] = (y * (gate * jax.nn.sigmoid(gate))).astype(jnp.bfloat16)


def in_vmem(count):
    return [pl.BlockSpec(memory_space=pltpu.VMEM)] * count


def local_states(low, dt_proj, dt_bias, act, alog, bc, prompts):
    rows, channels = act.shape
    groups = channels // LANES
    nst = alog.shape[0]
    body = lambda *refs: state_kernel(rows // prompts, prompts, nst, groups, *refs)
    f32 = jnp.float32
    return pl.pallas_call(
        body,
        out_shape=[
            jax.ShapeDtypeStruct((rows * groups, LANES), f32),
            jax.ShapeDtypeStruct((rows * groups, LANES), f32),
            jax.ShapeDtypeStruct((prompts, nst, groups, LANES), f32),
            jax.ShapeDtypeStruct((prompts, groups, LANES), f32),
        ],
        in_specs=in_vmem(5) + [pl.BlockSpec(memory_space=pltpu.SMEM)],
        out_specs=in_vmem(4),
        compiler_params=pltpu.CompilerParams(vmem_limit_bytes=VMEM_LIMIT),
        name="local_states",
    )(low, dt_proj, dt_bias, act, alog, bc)


def gated_output(dtx, actx, alog, bc, entering, skip, gate):
    rows, channels = gate.shape
    groups = channels // LANES
    prompts, nst = entering.shape[:2]
    body = lambda *refs: output_kernel(rows // prompts, prompts, nst, groups, *refs)
    return pl.pallas_call(
        body,
        out_shape=jax.ShapeDtypeStruct((rows, channels), jnp.bfloat16),
        in_specs=in_vmem(3) + [pl.BlockSpec(memory_space=pltpu.SMEM)] + in_vmem(3),
        out_specs=pl.BlockSpec(memory_space=pltpu.VMEM),
        scratch_shapes=[pltpu.VMEM((rows * groups, LANES), jnp.float32)],
        compiler_params=pltpu.CompilerParams(vmem_limit_bytes=VMEM_LIMIT),
        name="gated_output",
    )(dtx, actx, alog, bc, entering, skip, gate)


def entering_state(totals, states, alog, carry):
    place = lax.axis_index("seq")
    rate = -jnp.exp(alog)
    state = carry
    for j in range(totals.shape[0]):
        later = jnp.exp(rate[None] * totals[j][:, None]) * state + states[j]
        state = jnp.where(j < place, later, state)
    return state


def shards(
    layer_input,
    x_branch,
    gate_branch,
    conv_weight,
    conv_bias,
    x_proj,
    dt_proj,
    dt_bias,
    a_log,
    d_skip,
    carry_state,
    carry_tail,
    out_proj,
    steering,
    refusal,
    norm_gain,
    router,
    specialist_switch_matrix,
    w_up,
    w_down,
    expert_ids,
):
    width = conv_weight.shape[0] - 1
    length, prompts, channels = x_branch.shape
    groups = channels // LANES
    received = passed_along(x_branch[length - width :], "seq", 1)
    leading_shard = lax.axis_index("seq") == 0
    tail = jnp.where(leading_shard, carry_tail, received)
    padded = jnp.concatenate([tail, x_branch], axis=0).astype(jnp.float32)
    convolved = conv_bias.astype(jnp.float32)
    for k in range(conv_weight.shape[0]):
        convolved = convolved + conv_weight[k].astype(jnp.float32) * padded[k : k + length]
    row_count = length * prompts
    activated = jax.nn.silu(convolved).reshape(row_count, channels)
    flat_act = activated.astype(jnp.bfloat16)
    projected = lax.psum(jnp.dot(flat_act, x_proj, preferred_element_type=jnp.float32), "expert")
    low_rank = dt_proj.shape[0]
    state_size = a_log.shape[1]
    low = projected[:, :low_rank].astype(jnp.bfloat16)
    bc = projected[:, low_rank:].reshape(-1)
    alog = a_log.T.reshape(state_size, groups, LANES)
    dtx, actx, state, total = local_states(
        low, dt_proj, dt_bias.reshape(1, channels), activated, alog, bc, prompts
    )
    sent = jnp.concatenate([total[:, None], state], axis=1)
    gathered = lax.all_gather(sent, "seq")
    carry = carry_state.transpose(0, 2, 1).reshape(prompts, state_size, groups, LANES)
    entering = entering_state(gathered[:, :, 0], gathered[:, :, 1:], alog, carry)
    gated = gated_output(
        dtx, actx, alog, bc, entering, d_skip.reshape(groups, LANES), gate_branch.reshape(row_count, channels)
    )
    d_model = out_proj.shape[1]
    mixed = jnp.dot(gated, out_proj, preferred_element_type=jnp.float32)
    steering_clean = remove_directions(steering, refusal)
    owner = lax.axis_index("expert")
    own_length = layer_input.shape[0]
    top_count = expert_ids.shape[-1]
    experts = router.shape[1]
    capacity = row_count * top_count * 5 // (4 * experts)
    row_ids = expert_ids.reshape(row_count, top_count)
    slots = slot_matrix(row_ids, owner, capacity)
    slots16 = slots.astype(jnp.bfloat16)
    own_mixed = lax.psum_scatter(
        mixed.astype(jnp.bfloat16), "expert", scatter_dimension=0, tiled=True
    ).astype(jnp.float32)
    own_residual = (
        layer_input.astype(jnp.float32).reshape(own_length * prompts, d_model) + own_mixed + steering_clean
    )
    own_normed = root_mean_normed(own_residual, norm_gain)
    normed = lax.all_gather(own_normed, "expert", axis=0, tiled=True)
    weight_rows = owner_weight(normed, router, row_ids, owner)
    expert_in = jnp.dot(slots16, normed, preferred_element_type=jnp.float32).astype(jnp.bfloat16)
    slot_weight = jnp.sum(jnp.where(slots, weight_rows[None, :], 0.0), axis=1)
    pieces = lax.all_gather(expert_in, "seq", axis=0, tiled=True)
    gate = jnp.dot(pieces, specialist_switch_matrix[0], preferred_element_type=jnp.float32)
    upward = jnp.dot(pieces, w_up[0], preferred_element_type=jnp.float32)
    hidden = (jax.nn.silu(gate) * upward).astype(jnp.bfloat16)
    expert_out = lax.psum_scatter(
        jnp.dot(hidden, w_down[0], preferred_element_type=jnp.float32).astype(jnp.bfloat16),
        "seq",
        scatter_dimension=0,
        tiled=True,
    ).astype(jnp.float32)
    weighted = (expert_out * slot_weight[:, None]).astype(jnp.bfloat16)
    spread = jnp.dot(slots16.T, weighted, preferred_element_type=jnp.float32).astype(jnp.bfloat16)
    combined = lax.psum_scatter(spread, "expert", scatter_dimension=0, tiled=True)
    return (own_residual + combined.astype(jnp.float32)).reshape(own_length, prompts, d_model)


def solution(mesh):
    return jax.shard_map(
        shards,
        mesh=mesh,
        in_specs=(
            P(("seq", "expert"), None, None),
            P("seq", None, "expert"),
            P("seq", None, "expert"),
            P(None, "expert"),
            P("expert"),
            P("expert", None),
            P(None, "expert"),
            P("expert"),
            P("expert", None),
            P("expert"),
            P(None, "expert", None),
            P(None, None, "expert"),
            P("expert", None),
            P(),
            P(),
            P(),
            P(),
            P("expert", None, "seq"),
            P("expert", None, "seq"),
            P("expert", "seq", None),
            P("seq", None, None),
        ),
        out_specs=P(("seq", "expert"), None, None),
        check_vma=False,
    )
```

```python
import jax
import jax.numpy as jnp
from jax import lax
from jax.experimental import pallas as pl
from jax.experimental.pallas import tpu as pltpu
from jax.sharding import PartitionSpec as P

EPS = 1e-06
VMEM_LIMIT = 48 * 1024 * 1024
LANES = 128


def passed_along(array, axis, by):
    count = lax.axis_size(axis)
    pairs = [(i, i + by) for i in range(count) if 0 <= i + by < count]
    return lax.ppermute(array, axis, pairs)


def remove_directions(steering, refusal):
    vector = steering.astype(jnp.float32)
    units = []
    for k in range(refusal.shape[0]):
        r = refusal[k].astype(jnp.float32)
        for q in units:
            r = r - jnp.sum(q * r) * q
        r = r * lax.rsqrt(jnp.sum(r * r) + EPS)
        units.append(r)
    for q in units:
        vector = vector - jnp.sum(q * vector) * q
    return vector


def root_mean_normed(residual, norm_gain):
    scaled = residual * lax.rsqrt(jnp.mean(residual * residual, axis=-1, keepdims=True) + EPS)
    return (scaled * norm_gain.astype(jnp.float32)).astype(jnp.bfloat16)


def owner_weight(normed, router, picked_indices, owner):
    experts = router.shape[1]
    logits = jnp.dot(normed, router, preferred_element_type=jnp.float32)
    labels = jnp.arange(experts, dtype=jnp.int32)
    onehot = (picked_indices[:, :, None] == labels[None, None, :]).astype(jnp.float32)
    picked = jnp.sum(onehot * logits[:, None, :], axis=-1)
    leading = jax.nn.sigmoid(picked[:, 0] - picked[:, 1])
    shares = jnp.stack([leading, 1.0 - leading], axis=1)
    per_expert = jnp.sum(onehot * shares[:, :, None], axis=1)
    return jnp.sum(per_expert * (labels == owner).astype(jnp.float32)[None, :], axis=1)


def slot_matrix(picked_indices, owner, capacity):
    member = jnp.any(picked_indices == owner, axis=1)
    order = jnp.cumsum(member.astype(jnp.int32)) - 1
    slots = jnp.arange(capacity, dtype=jnp.int32)
    return (order[None, :] == slots[:, None]) & member[None, :]


def state_kernel(length, prompts, nst, groups, low_ref, dtp_ref, dtb_ref, act_ref, alog_ref, b_ref,
                 dtx_ref, actx_ref, state_ref, total_ref):
    rows = length * prompts
    for k in range(groups):
        cols = pl.ds(k * LANES, LANES)
        raw = jnp.dot(low_ref[...], dtp_ref[:, cols], preferred_element_type=jnp.float32)
        dtx_ref[pl.ds(k, rows, stride=groups), :] = jax.nn.softplus(raw + dtb_ref[:, cols])
        actx_ref[pl.ds(k, rows, stride=groups), :] = act_ref[:, cols]
    rates = [-jnp.exp(alog_ref[n]) for n in range(nst)]
    for p in range(prompts):

        def step(t, carry):
            states, total = carry
            row = t * prompts + p
            at = pl.ds(pl.multiple_of(row * groups, groups), groups)
            dt = dtx_ref[at, :]
            drive = dt * actx_ref[at, :]
            states = tuple(
                jnp.exp(dt * rates[n]) * states[n] + drive * b_ref[row * 2 * nst + n]
                for n in range(nst)
            )
            return states, total + dt

        zero = jnp.zeros((groups, LANES), jnp.float32)
        states, total = lax.fori_loop(0, length, step, ((zero,) * nst, zero), unroll=4)
        for n in range(nst):
            state_ref[p, n] = states[n]
        total_ref[p] = total


def output_kernel(length, prompts, nst, groups, dtx_ref, actx_ref, alog_ref, b_ref, enter_ref, skip_ref,
                  gate_ref, out_ref, y_ref):
    rows = length * prompts
    rates = [-jnp.exp(alog_ref[n]) for n in range(nst)]
    skip = skip_ref[...]
    for p in range(prompts):

        def step(t, states):
            row = t * prompts + p
            at = pl.ds(pl.multiple_of(row * groups, groups), groups)
            dt = dtx_ref[at, :]
            act = actx_ref[at, :]
            drive = dt * act
            y = skip * act
            fresh = []
            for n in range(nst):
                s = jnp.exp(dt * rates[n]) * states[n] + drive * b_ref[row * 2 * nst + n]
                y = y + s * b_ref[row * 2 * nst + nst + n]
                fresh.append(s)
            y_ref[at, :] = y
            return tuple(fresh)

        lax.fori_loop(0, length, step, tuple(enter_ref[p, n] for n in range(nst)), unroll=4)
    for k in range(groups):
        cols = pl.ds(k * LANES, LANES)
        gate = gate_ref[:, cols].astype(jnp.float32)
        y = y_ref[pl.ds(k, rows, stride=groups), :]
        out_ref[:, cols] = (y * (gate * jax.nn.sigmoid(gate))).astype(jnp.bfloat16)


def in_vmem(count):
    return [pl.BlockSpec(memory_space=pltpu.VMEM)] * count


def local_states(low, dt_proj, dt_bias, act, alog, bc, prompts):
    rows, channels = act.shape
    groups = channels // LANES
    nst = alog.shape[0]
    body = lambda *refs: state_kernel(rows // prompts, prompts, nst, groups, *refs)
    f32 = jnp.float32
    return pl.pallas_call(
        body,
        out_shape=[
            jax.ShapeDtypeStruct((rows * groups, LANES), f32),
            jax.ShapeDtypeStruct((rows * groups, LANES), f32),
            jax.ShapeDtypeStruct((prompts, nst, groups, LANES), f32),
            jax.ShapeDtypeStruct((prompts, groups, LANES), f32),
        ],
        in_specs=in_vmem(5) + [pl.BlockSpec(memory_space=pltpu.SMEM)],
        out_specs=in_vmem(4),
        compiler_params=pltpu.CompilerParams(vmem_limit_bytes=VMEM_LIMIT),
        name="local_states",
    )(low, dt_proj, dt_bias, act, alog, bc)


def gated_output(dtx, actx, alog, bc, entering, skip, gate):
    rows, channels = gate.shape
    groups = channels // LANES
    prompts, nst = entering.shape[:2]
    body = lambda *refs: output_kernel(rows // prompts, prompts, nst, groups, *refs)
    return pl.pallas_call(
        body,
        out_shape=jax.ShapeDtypeStruct((rows, channels), jnp.bfloat16),
        in_specs=in_vmem(3) + [pl.BlockSpec(memory_space=pltpu.SMEM)] + in_vmem(3),
        out_specs=pl.BlockSpec(memory_space=pltpu.VMEM),
        scratch_shapes=[pltpu.VMEM((rows * groups, LANES), jnp.float32)],
        compiler_params=pltpu.CompilerParams(vmem_limit_bytes=VMEM_LIMIT),
        name="gated_output",
    )(dtx, actx, alog, bc, entering, skip, gate)


def greet(devices):
    barrier = pltpu.get_barrier_semaphore()
    for device in devices:
        pl.semaphore_signal(barrier, inc=1, device_id=device, device_id_type=pl.DeviceIdType.MESH)
    pl.semaphore_wait(barrier, len(devices))


def push(source, target, sends, receives, slot, device):
    return pltpu.make_async_remote_copy(
        src_ref=source,
        dst_ref=target,
        send_sem=sends.at[slot],
        recv_sem=receives.at[slot],
        device_id=device,
        device_id_type=pl.DeviceIdType.MESH,
    )


def chip_places(seq_count):
    chips = seq_count // 2
    place = lax.axis_index("seq")
    expert = lax.axis_index("expert")
    chip = place // 2
    core = place % 2
    sibling = (chip * 2 + 1 - core, expert)

    def ahead(step):
        return ((chip + step) % chips * 2 + core, expert)

    return chips, chip, core, sibling, ahead


def expert_sum_kernel(count, part_ref, out_ref, got, send_a, recv_a, send_b, recv_b):
    place = lax.axis_index("seq")
    me = lax.axis_index("expert")
    block = part_ref.shape[0] // count
    peers = [((place, (me + r) % count), (me + r) % count) for r in range(1, count)]
    greet([device for device, _ in peers])
    mine = pl.ds(pl.multiple_of(me * block, block), block)
    first = []
    for r, (device, other) in enumerate(peers):
        rows = pl.ds(pl.multiple_of(other * block, block), block)
        copy = push(part_ref.at[rows], got.at[r], send_a, recv_a, r, device)
        copy.start()
        first.append(copy)
    total = part_ref[mine, :]
    for r, copy in enumerate(first):
        copy.wait_recv()
        total = total + got[r]
    out_ref[mine, :] = total
    second = []
    for r, (device, _) in enumerate(peers):
        copy = push(out_ref.at[mine], out_ref.at[mine], send_b, recv_b, r, device)
        copy.start()
        second.append(copy)
    for copy in second:
        copy.wait_recv()
    for copy in first + second:
        copy.wait_send()


def expert_sum(part):
    count = lax.axis_size("expert")
    rows, width = part.shape
    dma = pltpu.SemaphoreType.DMA((count - 1,))
    return pl.pallas_call(
        lambda *refs: expert_sum_kernel(count, *refs),
        out_shape=jax.ShapeDtypeStruct(part.shape, part.dtype),
        in_specs=in_vmem(1),
        out_specs=pl.BlockSpec(memory_space=pltpu.VMEM),
        scratch_shapes=[pltpu.VMEM((count - 1, rows // count, width), part.dtype)] + [dma] * 4,
        compiler_params=pltpu.CompilerParams(
            collective_id=0, has_side_effects=True, vmem_limit_bytes=VMEM_LIMIT
        ),
        name="expert_sum",
    )(part)


def state_gather_kernel(seq_count, part_ref, out_ref, send_x, recv_x, send_f, recv_f):
    chips, chip, core, sibling, ahead = chip_places(seq_count)
    greet([sibling] + [ahead(r) for r in range(1, chips)])
    me = chip * 2 + core
    copies = []
    for r in range(1, chips):
        copy = push(part_ref, out_ref.at[me], send_x, recv_x, r, ahead(r))
        copy.start()
        copies.append(copy)
    forward = push(part_ref, out_ref.at[me], send_f, recv_f, 0, sibling)
    forward.start()
    forwards = [forward]
    out_ref[me] = part_ref[...]
    for r in range(1, chips):
        copies[r - 1].wait_recv()
        source = (chip - r + chips) % chips * 2 + core
        forward = push(out_ref.at[source], out_ref.at[source], send_f, recv_f, r, sibling)
        forward.start()
        forwards.append(forward)
    for forward in forwards:
        forward.wait_recv()
    for copy in copies + forwards:
        copy.wait_send()


def state_gather(part):
    seq_count = lax.axis_size("seq")
    dma = pltpu.SemaphoreType.DMA((seq_count // 2,))
    return pl.pallas_call(
        lambda *refs: state_gather_kernel(seq_count, *refs),
        out_shape=jax.ShapeDtypeStruct((seq_count,) + part.shape, part.dtype),
        in_specs=in_vmem(1),
        out_specs=pl.BlockSpec(memory_space=pltpu.VMEM),
        scratch_shapes=[dma] * 4,
        compiler_params=pltpu.CompilerParams(
            collective_id=1, has_side_effects=True, vmem_limit_bytes=VMEM_LIMIT
        ),
        name="state_gather",
    )(part)


def experts_kernel(seq_count, x_ref, gate_ref, up_ref, down_ref, out_ref, pieces, mine, theirs, beside,
                   arrived, send_x, recv_x, send_f, recv_f, send_p, recv_p, send_o, recv_o):
    chips, chip, core, sibling, ahead = chip_places(seq_count)
    cap, d_model = x_ref.shape
    chunk = 512
    greet([sibling] + [ahead(r) for r in range(1, chips)])

    def tokens(r):
        return push(x_ref, pieces.at[r, 0], send_x, recv_x, r, ahead(r))

    def handed(r):
        return push(pieces.at[r, 0], pieces.at[r, 1], send_f, recv_f, r, sibling)

    def within(r):
        return push(theirs.at[r], beside.at[r], send_p, recv_p, r, sibling)

    def back(r):
        return push(mine.at[r], arrived.at[r], send_o, recv_o, r, ahead(chips - r))

    for r in range(1, chips):
        tokens(r).start()
    pieces[0, 0] = x_ref[...]
    handed(0).start()

    def compute(r):
        rows = pieces[r].reshape(2 * cap, d_model)
        gate = jnp.dot(rows, gate_ref[...], preferred_element_type=jnp.float32)
        upward = jnp.dot(rows, up_ref[...], preferred_element_type=jnp.float32)
        hidden = (gate * jax.nn.sigmoid(gate) * upward).astype(jnp.bfloat16)

        def columns(j, _):
            cols = pl.ds(pl.multiple_of(j * chunk, chunk), chunk)
            part = jnp.dot(hidden, down_ref[:, cols], preferred_element_type=jnp.float32).astype(
                jnp.bfloat16
            )
            mine[r, :, cols] = part[:cap]
            theirs[r, :, cols] = part[cap:]
            return 0

        lax.fori_loop(0, d_model // chunk, columns, 0)
        within(r).start()

    handed(0).wait_recv()
    compute(0)

    def turn(r, _):
        tokens(r).wait_recv()
        handed(r).start()
        handed(r).wait_recv()
        compute(r)
        within(r).wait_recv()

        def add(j, _):
            cols = pl.ds(pl.multiple_of(j * chunk, chunk), chunk)
            total = mine[r, :, cols].astype(jnp.float32) + beside[r, :, cols].astype(jnp.float32)
            mine[r, :, cols] = total.astype(jnp.bfloat16)
            return 0

        lax.fori_loop(0, d_model // chunk, add, 0)
        back(r).start()
        return 0

    lax.fori_loop(1, chips, turn, 0)
    within(0).wait_recv()
    for r in range(1, chips):
        back(r).wait_recv()

    def finish(j, _):
        cols = pl.ds(pl.multiple_of(j * chunk, chunk), chunk)
        total = mine[0, :, cols].astype(jnp.float32) + beside[0, :, cols].astype(jnp.float32)
        for r in range(1, chips):
            total = total + arrived[r, :, cols].astype(jnp.float32)
        out_ref[:, cols] = total
        return 0

    lax.fori_loop(0, d_model // chunk, finish, 0)
    for r in range(chips):
        handed(r).wait_send()
        within(r).wait_send()
        if r > 0:
            tokens(r).wait_send()
            back(r).wait_send()


def run_experts(x, gate, up, down):
    seq_count = lax.axis_size("seq")
    chips = seq_count // 2
    cap, d_model = x.shape
    dma = pltpu.SemaphoreType.DMA((chips,))
    block = pltpu.VMEM((chips, cap, d_model), jnp.bfloat16)
    return pl.pallas_call(
        lambda *refs: experts_kernel(seq_count, *refs),
        out_shape=jax.ShapeDtypeStruct((cap, d_model), jnp.float32),
        in_specs=in_vmem(4),
        out_specs=pl.BlockSpec(memory_space=pltpu.VMEM),
        scratch_shapes=[pltpu.VMEM((chips, 2, cap, d_model), jnp.bfloat16)] + [block] * 4 + [dma] * 8,
        compiler_params=pltpu.CompilerParams(
            collective_id=2, has_side_effects=True, vmem_limit_bytes=60 * 1024 * 1024
        ),
        name="experts",
    )(x, gate, up, down)


def entering_state(totals, states, alog, carry):
    place = lax.axis_index("seq")
    rate = -jnp.exp(alog)
    state = carry
    for j in range(totals.shape[0]):
        later = jnp.exp(rate[None] * totals[j][:, None]) * state + states[j]
        state = jnp.where(j < place, later, state)
    return state


def shards(
    layer_input,
    x_branch,
    gate_branch,
    conv_weight,
    conv_bias,
    x_proj,
    dt_proj,
    dt_bias,
    a_log,
    d_skip,
    carry_state,
    carry_tail,
    out_proj,
    steering,
    refusal,
    norm_gain,
    router,
    specialist_switch_matrix,
    w_up,
    w_down,
    expert_ids,
):
    width = conv_weight.shape[0] - 1
    length, prompts, channels = x_branch.shape
    groups = channels // LANES
    received = passed_along(x_branch[length - width :], "seq", 1)
    leading_shard = lax.axis_index("seq") == 0
    tail = jnp.where(leading_shard, carry_tail, received)
    padded = jnp.concatenate([tail, x_branch], axis=0).astype(jnp.float32)
    convolved = conv_bias.astype(jnp.float32)
    for k in range(conv_weight.shape[0]):
        convolved = convolved + conv_weight[k].astype(jnp.float32) * padded[k : k + length]
    row_count = length * prompts
    activated = jax.nn.silu(convolved).reshape(row_count, channels)
    flat_act = activated.astype(jnp.bfloat16)
    projected = expert_sum(jnp.dot(flat_act, x_proj, preferred_element_type=jnp.float32))
    low_rank = dt_proj.shape[0]
    state_size = a_log.shape[1]
    low = projected[:, :low_rank].astype(jnp.bfloat16)
    bc = projected[:, low_rank:].reshape(-1)
    alog = a_log.T.reshape(state_size, groups, LANES)
    dtx, actx, state, total = local_states(
        low, dt_proj, dt_bias.reshape(1, channels), activated, alog, bc, prompts
    )
    sent = jnp.concatenate([total[:, None], state], axis=1)
    gathered = state_gather(sent)
    carry = carry_state.transpose(0, 2, 1).reshape(prompts, state_size, groups, LANES)
    entering = entering_state(gathered[:, :, 0], gathered[:, :, 1:], alog, carry)
    gated = gated_output(
        dtx, actx, alog, bc, entering, d_skip.reshape(groups, LANES), gate_branch.reshape(row_count, channels)
    )
    d_model = out_proj.shape[1]
    mixed = jnp.dot(gated, out_proj, preferred_element_type=jnp.float32)
    steering_clean = remove_directions(steering, refusal)
    owner = lax.axis_index("expert")
    own_length = layer_input.shape[0]
    top_count = expert_ids.shape[-1]
    experts = router.shape[1]
    capacity = row_count * top_count * 5 // (4 * experts)
    capacity = (capacity + 15) // 16 * 16
    row_ids = expert_ids.reshape(row_count, top_count)
    slots = slot_matrix(row_ids, owner, capacity)
    slots16 = slots.astype(jnp.bfloat16)
    own_mixed = lax.psum_scatter(
        mixed.astype(jnp.bfloat16), "expert", scatter_dimension=0, tiled=True
    ).astype(jnp.float32)
    own_residual = (
        layer_input.astype(jnp.float32).reshape(own_length * prompts, d_model) + own_mixed + steering_clean
    )
    own_normed = root_mean_normed(own_residual, norm_gain)
    normed = lax.all_gather(own_normed, "expert", axis=0, tiled=True)
    weight_rows = owner_weight(normed, router, row_ids, owner)
    expert_in = jnp.dot(slots16, normed, preferred_element_type=jnp.float32).astype(jnp.bfloat16)
    slot_weight = jnp.sum(jnp.where(slots, weight_rows[None, :], 0.0), axis=1)
    expert_out = run_experts(expert_in, specialist_switch_matrix[0], w_up[0], w_down[0])
    weighted = (expert_out * slot_weight[:, None]).astype(jnp.bfloat16)
    spread = jnp.dot(slots16.T, weighted, preferred_element_type=jnp.float32).astype(jnp.bfloat16)
    combined = lax.psum_scatter(spread, "expert", scatter_dimension=0, tiled=True)
    return (own_residual + combined.astype(jnp.float32)).reshape(own_length, prompts, d_model)


def solution(mesh):
    return jax.shard_map(
        shards,
        mesh=mesh,
        in_specs=(
            P(("seq", "expert"), None, None),
            P("seq", None, "expert"),
            P("seq", None, "expert"),
            P(None, "expert"),
            P("expert"),
            P("expert", None),
            P(None, "expert"),
            P("expert"),
            P("expert", None),
            P("expert"),
            P(None, "expert", None),
            P(None, None, "expert"),
            P("expert", None),
            P(),
            P(),
            P(),
            P(),
            P("expert", None, "seq"),
            P("expert", None, "seq"),
            P("expert", "seq", None),
            P("seq", None, None),
        ),
        out_specs=P(("seq", "expert"), None, None),
        check_vma=False,
    )
```

```python
import jax
import jax.numpy as jnp
from jax import lax
from jax.experimental import pallas as pl
from jax.experimental.pallas import tpu as pltpu
from jax.sharding import PartitionSpec as P

EPS = 1e-06
VMEM_LIMIT = 48 * 1024 * 1024
LANES = 128


def passed_along(array, axis, by):
    count = lax.axis_size(axis)
    pairs = [(i, i + by) for i in range(count) if 0 <= i + by < count]
    return lax.ppermute(array, axis, pairs)


def remove_directions(steering, refusal):
    vector = steering.astype(jnp.float32)
    units = []
    for direction in refusal:
        r = direction.astype(jnp.float32)
        for q in units:
            r = r - jnp.sum(q * r) * q
        r = r * lax.rsqrt(jnp.sum(r * r) + EPS)
        units.append(r)
    for q in units:
        vector = vector - jnp.sum(q * vector) * q
    return vector


def owner_weight(normed, router, picked_indices, owner):
    experts = router.shape[1]
    logits = jnp.dot(normed, router, preferred_element_type=jnp.float32)
    labels = jnp.arange(experts, dtype=jnp.int32)
    onehot = (picked_indices[:, :, None] == labels[None, None, :]).astype(jnp.float32)
    picked = jnp.sum(onehot * logits[:, None, :], axis=-1)
    leading = jax.nn.sigmoid(picked[:, 0] - picked[:, 1])
    shares = jnp.stack([leading, 1.0 - leading], axis=1)
    per_expert = jnp.sum(onehot * shares[:, :, None], axis=1)
    return jnp.sum(per_expert * (labels == owner).astype(jnp.float32)[None, :], axis=1)


def slot_matrix(picked_indices, owner, capacity):
    member = jnp.any(picked_indices == owner, axis=1)
    order = jnp.cumsum(member.astype(jnp.int32)) - 1
    slots = jnp.arange(capacity, dtype=jnp.int32)
    return (order[None, :] == slots[:, None]) & member[None, :]


def state_kernel(length, prompts, nst, groups, low_ref, dtp_ref, dtb_ref, act_ref, alog_ref, b_ref,
                 dtx_ref, actx_ref, state_ref, total_ref):
    rows = length * prompts
    for k in range(groups):
        cols = pl.ds(k * LANES, LANES)
        raw = jnp.dot(low_ref[...], dtp_ref[:, cols], preferred_element_type=jnp.float32)
        dtx_ref[pl.ds(k, rows, stride=groups), :] = jax.nn.softplus(raw + dtb_ref[:, cols])
        actx_ref[pl.ds(k, rows, stride=groups), :] = act_ref[:, cols]
    rates = [-jnp.exp(alog_ref[n]) for n in range(nst)]
    for p in range(prompts):

        def step(t, carry):
            states, total = carry
            row = t * prompts + p
            at = pl.ds(pl.multiple_of(row * groups, groups), groups)
            dt = dtx_ref[at, :]
            drive = dt * actx_ref[at, :]
            states = tuple(
                jnp.exp(dt * rates[n]) * states[n] + drive * b_ref[row * 2 * nst + n]
                for n in range(nst)
            )
            return states, total + dt

        zero = jnp.zeros((groups, LANES), jnp.float32)
        states, total = lax.fori_loop(0, length, step, ((zero,) * nst, zero), unroll=4)
        for n in range(nst):
            state_ref[p, n] = states[n]
        total_ref[p] = total


def output_kernel(length, prompts, nst, groups, dtx_ref, actx_ref, alog_ref, b_ref, enter_ref, skip_ref,
                  gate_ref, out_ref, y_ref):
    rows = length * prompts
    rates = [-jnp.exp(alog_ref[n]) for n in range(nst)]
    skip = skip_ref[...]
    for p in range(prompts):

        def step(t, states):
            row = t * prompts + p
            at = pl.ds(pl.multiple_of(row * groups, groups), groups)
            dt = dtx_ref[at, :]
            act = actx_ref[at, :]
            drive = dt * act
            y = skip * act
            fresh = []
            for n in range(nst):
                s = jnp.exp(dt * rates[n]) * states[n] + drive * b_ref[row * 2 * nst + n]
                y = y + s * b_ref[row * 2 * nst + nst + n]
                fresh.append(s)
            y_ref[at, :] = y
            return tuple(fresh)

        lax.fori_loop(0, length, step, tuple(enter_ref[p, n] for n in range(nst)), unroll=4)
    for k in range(groups):
        cols = pl.ds(k * LANES, LANES)
        gate = gate_ref[:, cols].astype(jnp.float32)
        y = y_ref[pl.ds(k, rows, stride=groups), :]
        out_ref[:, cols] = (y * (gate * jax.nn.sigmoid(gate))).astype(jnp.bfloat16)


def in_vmem(count):
    return [pl.BlockSpec(memory_space=pltpu.VMEM)] * count


def local_states(low, dt_proj, dt_bias, act, alog, bc, prompts):
    rows, channels = act.shape
    groups = channels // LANES
    nst = alog.shape[0]
    body = lambda *refs: state_kernel(rows // prompts, prompts, nst, groups, *refs)
    f32 = jnp.float32
    return pl.pallas_call(
        body,
        out_shape=[
            jax.ShapeDtypeStruct((rows * groups, LANES), f32),
            jax.ShapeDtypeStruct((rows * groups, LANES), f32),
            jax.ShapeDtypeStruct((prompts, nst, groups, LANES), f32),
            jax.ShapeDtypeStruct((prompts, groups, LANES), f32),
        ],
        in_specs=in_vmem(5) + [pl.BlockSpec(memory_space=pltpu.SMEM)],
        out_specs=in_vmem(4),
        compiler_params=pltpu.CompilerParams(vmem_limit_bytes=VMEM_LIMIT),
        name="local_states",
    )(low, dt_proj, dt_bias, act, alog, bc)


def gated_output(dtx, actx, alog, bc, entering, skip, gate):
    rows, channels = gate.shape
    groups = channels // LANES
    prompts, nst = entering.shape[:2]
    body = lambda *refs: output_kernel(rows // prompts, prompts, nst, groups, *refs)
    return pl.pallas_call(
        body,
        out_shape=jax.ShapeDtypeStruct((rows, channels), jnp.bfloat16),
        in_specs=in_vmem(3) + [pl.BlockSpec(memory_space=pltpu.SMEM)] + in_vmem(3),
        out_specs=pl.BlockSpec(memory_space=pltpu.VMEM),
        scratch_shapes=[pltpu.VMEM((rows * groups, LANES), jnp.float32)],
        compiler_params=pltpu.CompilerParams(vmem_limit_bytes=VMEM_LIMIT),
        name="gated_output",
    )(dtx, actx, alog, bc, entering, skip, gate)


def greet(devices):
    barrier = pltpu.get_barrier_semaphore()
    for device in devices:
        pl.semaphore_signal(barrier, inc=1, device_id=device, device_id_type=pl.DeviceIdType.MESH)
    pl.semaphore_wait(barrier, len(devices))


def push(source, target, sends, receives, slot, device):
    return pltpu.make_async_remote_copy(
        src_ref=source,
        dst_ref=target,
        send_sem=sends.at[slot],
        recv_sem=receives.at[slot],
        device_id=device,
        device_id_type=pl.DeviceIdType.MESH,
    )


def chip_places(seq_count):
    chips = seq_count // 2
    place = lax.axis_index("seq")
    expert = lax.axis_index("expert")
    chip = place // 2
    core = place % 2
    sibling = (chip * 2 + 1 - core, expert)

    def ahead(step):
        return ((chip + step) % chips * 2 + core, expert)

    return chips, chip, core, sibling, ahead


def expert_sum_kernel(count, part_ref, out_ref, got, send_a, recv_a, send_b, recv_b):
    place = lax.axis_index("seq")
    me = lax.axis_index("expert")
    block = part_ref.shape[0] // count
    peers = [((place, (me + r) % count), (me + r) % count) for r in range(1, count)]
    greet([device for device, _ in peers])
    mine = pl.ds(pl.multiple_of(me * block, block), block)
    first = []
    for r, (device, other) in enumerate(peers):
        rows = pl.ds(pl.multiple_of(other * block, block), block)
        copy = push(part_ref.at[rows], got.at[r], send_a, recv_a, r, device)
        copy.start()
        first.append(copy)
    total = part_ref[mine, :]
    for r, copy in enumerate(first):
        copy.wait_recv()
        total = total + got[r]
    out_ref[mine, :] = total
    second = []
    for r, (device, _) in enumerate(peers):
        copy = push(out_ref.at[mine], out_ref.at[mine], send_b, recv_b, r, device)
        copy.start()
        second.append(copy)
    for copy in second:
        copy.wait_recv()
    for copy in first + second:
        copy.wait_send()


def expert_sum(part):
    count = lax.axis_size("expert")
    rows, width = part.shape
    dma = pltpu.SemaphoreType.DMA((count - 1,))
    return pl.pallas_call(
        lambda *refs: expert_sum_kernel(count, *refs),
        out_shape=jax.ShapeDtypeStruct(part.shape, part.dtype),
        in_specs=in_vmem(1),
        out_specs=pl.BlockSpec(memory_space=pltpu.VMEM),
        scratch_shapes=[pltpu.VMEM((count - 1, rows // count, width), part.dtype)] + [dma] * 4,
        compiler_params=pltpu.CompilerParams(
            collective_id=0, has_side_effects=True, vmem_limit_bytes=VMEM_LIMIT
        ),
        name="expert_sum",
    )(part)


def state_gather_kernel(seq_count, part_ref, out_ref, send_x, recv_x, send_f, recv_f):
    chips, chip, core, sibling, ahead = chip_places(seq_count)
    greet([sibling] + [ahead(r) for r in range(1, chips)])
    me = chip * 2 + core
    copies = []
    for r in range(1, chips):
        copy = push(part_ref, out_ref.at[me], send_x, recv_x, r, ahead(r))
        copy.start()
        copies.append(copy)
    forward = push(part_ref, out_ref.at[me], send_f, recv_f, 0, sibling)
    forward.start()
    forwards = [forward]
    out_ref[me] = part_ref[...]
    for r in range(1, chips):
        copies[r - 1].wait_recv()
        source = (chip - r + chips) % chips * 2 + core
        forward = push(out_ref.at[source], out_ref.at[source], send_f, recv_f, r, sibling)
        forward.start()
        forwards.append(forward)
    for forward in forwards:
        forward.wait_recv()
    for copy in copies + forwards:
        copy.wait_send()


def state_gather(part):
    seq_count = lax.axis_size("seq")
    dma = pltpu.SemaphoreType.DMA((seq_count // 2,))
    return pl.pallas_call(
        lambda *refs: state_gather_kernel(seq_count, *refs),
        out_shape=jax.ShapeDtypeStruct((seq_count,) + part.shape, part.dtype),
        in_specs=in_vmem(1),
        out_specs=pl.BlockSpec(memory_space=pltpu.VMEM),
        scratch_shapes=[dma] * 4,
        compiler_params=pltpu.CompilerParams(
            collective_id=1, has_side_effects=True, vmem_limit_bytes=VMEM_LIMIT
        ),
        name="state_gather",
    )(part)


def experts_kernel(seq_count, x_ref, gate_ref, up_ref, down_ref, out_ref, pieces, mine, theirs, beside,
                   arrived, relay, send_x, recv_x, send_f, recv_f, send_p, recv_p, send_o, recv_o, send_d,
                   recv_d, send_e, recv_e, send_g, recv_g):
    chips, chip, core, sibling, ahead = chip_places(seq_count)
    expert = lax.axis_index("expert")
    cap, d_model = x_ref.shape
    half = d_model // 2
    chunk = 512
    square = chips == 4
    greet([sibling] + [ahead(r) for r in range(1, chips)])

    def onward(r):
        if not square:
            return ahead(r)
        other = {1: chip // 2 * 2 + 1 - chip % 2, 2: (chip + 2) % 4, 3: 3 - chip}[r]
        return (other * 2 + core, expert)

    def homeward(r):
        return onward(r) if square else ahead(chips - r)

    def halves(k):
        return pl.ds(k * half, half)

    def tokens(r):
        return push(x_ref, pieces.at[r, 0], send_x, recv_x, r, onward(r))

    def relayed(k):
        return push(pieces.at[1 + k, 0, :, halves(k)], pieces.at[3, 0, :, halves(k)], send_d, recv_d, k,
                    onward(2 - k))

    def handed(r):
        return push(pieces.at[r, 0], pieces.at[r, 1], send_f, recv_f, r, sibling)

    def within(r):
        return push(theirs.at[r], beside.at[r], send_p, recv_p, r, sibling)

    def back(r):
        return push(mine.at[r], arrived.at[r], send_o, recv_o, r, homeward(r))

    def back_first(k):
        return push(mine.at[3, :, halves(k)], relay.at[k], send_e, recv_e, k, onward(1 + k))

    def back_second(k):
        return push(relay.at[k], arrived.at[3, :, halves(k)], send_g, recv_g, k, onward(2 - k))

    near = (1, 2) if square else tuple(range(1, chips))
    for r in near:
        tokens(r).start()
    pieces[0, 0] = x_ref[...]
    handed(0).start()

    def compute(r):
        rows = pieces[r].reshape(2 * cap, d_model)
        gate = jnp.dot(rows, gate_ref[...], preferred_element_type=jnp.float32)
        upward = jnp.dot(rows, up_ref[...], preferred_element_type=jnp.float32)
        hidden = (gate * jax.nn.sigmoid(gate) * upward).astype(jnp.bfloat16)

        def columns(j, _):
            cols = pl.ds(pl.multiple_of(j * chunk, chunk), chunk)
            part = jnp.dot(hidden, down_ref[:, cols], preferred_element_type=jnp.float32).astype(
                jnp.bfloat16
            )
            mine[r, :, cols] = part[:cap]
            theirs[r, :, cols] = part[cap:]
            return 0

        lax.fori_loop(0, d_model // chunk, columns, 0)
        within(r).start()

    def chip_total(r):
        within(r).wait_recv()

        def add(j, _):
            cols = pl.ds(pl.multiple_of(j * chunk, chunk), chunk)
            total = mine[r, :, cols].astype(jnp.float32) + beside[r, :, cols].astype(jnp.float32)
            mine[r, :, cols] = total.astype(jnp.bfloat16)
            return 0

        lax.fori_loop(0, d_model // chunk, add, 0)

    handed(0).wait_recv()
    compute(0)
    if square:
        for r in near:
            tokens(r).wait_recv()
            relayed(r - 1).start()
            handed(r).start()
        for r in near:
            handed(r).wait_recv()
            compute(r)
            chip_total(r)
            back(r).start()
        for k in range(2):
            relayed(k).wait_recv()
        handed(3).start()
        handed(3).wait_recv()
        compute(3)
        chip_total(3)
        for k in range(2):
            back_first(k).start()
        for k in range(2):
            back_first(k).wait_recv()
            back_second(k).start()
    else:

        def turn(r, _):
            tokens(r).wait_recv()
            handed(r).start()
            handed(r).wait_recv()
            compute(r)
            chip_total(r)
            back(r).start()
            return 0

        lax.fori_loop(1, chips, turn, 0)
    within(0).wait_recv()
    for r in near:
        back(r).wait_recv()

    def finish(j, _):
        cols = pl.ds(pl.multiple_of(j * chunk, chunk), chunk)
        total = mine[0, :, cols].astype(jnp.float32) + beside[0, :, cols].astype(jnp.float32)
        for r in near:
            total = total + arrived[r, :, cols].astype(jnp.float32)
        out_ref[:, cols] = total
        return 0

    lax.fori_loop(0, d_model // chunk, finish, 0)
    if square:
        for k in range(2):
            back_second(k).wait_recv()
        out_ref[...] = out_ref[...] + arrived[3].astype(jnp.float32)
        for k in range(2):
            relayed(k).wait_send()
            back_first(k).wait_send()
            back_second(k).wait_send()
    for r in range(chips):
        handed(r).wait_send()
        within(r).wait_send()
    for r in near:
        tokens(r).wait_send()
        back(r).wait_send()


def run_experts(x, gate, up, down):
    seq_count = lax.axis_size("seq")
    chips = seq_count // 2
    cap, d_model = x.shape
    dma = pltpu.SemaphoreType.DMA((chips,))
    block = pltpu.VMEM((chips, cap, d_model), jnp.bfloat16)
    return pl.pallas_call(
        lambda *refs: experts_kernel(seq_count, *refs),
        out_shape=jax.ShapeDtypeStruct((cap, d_model), jnp.float32),
        in_specs=in_vmem(4),
        out_specs=pl.BlockSpec(memory_space=pltpu.VMEM),
        scratch_shapes=[pltpu.VMEM((chips, 2, cap, d_model), jnp.bfloat16)]
        + [block] * 4
        + [pltpu.VMEM((2, cap, d_model // 2), jnp.bfloat16)]
        + [dma] * 8
        + [pltpu.SemaphoreType.DMA((2,))] * 6,
        compiler_params=pltpu.CompilerParams(
            collective_id=2, has_side_effects=True, vmem_limit_bytes=60 * 1024 * 1024
        ),
        name="experts",
    )(x, gate, up, down)


def line_peers(count):
    place = lax.axis_index("seq")
    me = lax.axis_index("expert")
    return me, [((place, (me + r) % count), (me + r) % count) for r in range(1, count)]


def scattered_parts(left_ref, right_ref, part, got, sends, receives, peers, chunks):
    count = len(peers) + 1
    rows, d_model = part.shape
    block = rows // count
    width = d_model // chunks
    copies = []
    for j in range(chunks):
        cols = pl.ds(j * width, width)
        part[:, cols] = jnp.dot(
            left_ref[...], right_ref[:, cols], preferred_element_type=jnp.float32
        ).astype(jnp.bfloat16)
        for r, (device, other) in enumerate(peers):
            at = pl.ds(pl.multiple_of(other * block, block), block)
            copy = push(part.at[at, cols], got.at[r, :, cols], sends, receives, r * chunks + j, device)
            copy.start()
            copies.append(copy)
    return copies


def mix_kernel(count, chunks, gated_ref, proj_ref, input_ref, steer_ref, refusal_ref, gain_ref, residual_ref,
               normed_ref, part, got, send_a, recv_a, send_r, recv_r, send_l, recv_l):
    me, peers = line_peers(count)
    place = lax.axis_index("seq")
    block = input_ref.shape[0]
    d_model = input_ref.shape[1]
    greet([device for device, _ in peers])
    copies = scattered_parts(gated_ref, proj_ref, part, got, send_a, recv_a, peers, chunks)
    steering = remove_directions(steer_ref[...], [refusal_ref[k : k + 1, :] for k in range(refusal_ref.shape[0])])
    mine = pl.ds(pl.multiple_of(me * block, block), block)
    residual_ref[...] = (
        input_ref[...].astype(jnp.float32) + steering + part[mine, :].astype(jnp.float32)
    )
    for copy in copies:
        copy.wait_recv()
    width = d_model // chunks
    squares = jnp.zeros((block, 1), jnp.float32)
    for j in range(chunks):
        cols = pl.ds(j * width, width)
        total = residual_ref[:, cols]
        for r in range(count - 1):
            total = total + got[r, :, cols].astype(jnp.float32)
        residual_ref[:, cols] = total
        squares = squares + jnp.sum(total * total, axis=1, keepdims=True)
    scale = lax.rsqrt(squares / d_model + EPS)
    for j in range(chunks):
        cols = pl.ds(j * width, width)
        normed_ref[mine, cols] = (
            residual_ref[:, cols] * scale * gain_ref[:, cols].astype(jnp.float32)
        ).astype(jnp.bfloat16)

    def moved(owner, sends, receives, step, by):
        at = pl.ds(pl.multiple_of(owner * block, block), block)
        device = (place, (me + by + count) % count)
        return push(normed_ref.at[at], normed_ref.at[at], sends, receives, step, device)

    def right(step):
        return moved((me - step + count) % count, send_r, recv_r, step, 1)

    def left(step):
        return moved((me + step) % count, send_l, recv_l, step, -1)

    for step in range(count):
        if step > 0:

            @pl.when(me >= step)
            def _():
                right(step - 1).wait_recv()

            @pl.when(me + step < count)
            def _():
                left(step - 1).wait_recv()

        if step < count - 1:

            @pl.when((me >= step) & (me + 1 < count))
            def _():
                right(step).start()

            @pl.when((me + step < count) & (me > 0))
            def _():
                left(step).start()

    for step in range(count - 1):

        @pl.when((me >= step) & (me + 1 < count))
        def _():
            right(step).wait_send()

        @pl.when((me + step < count) & (me > 0))
        def _():
            left(step).wait_send()

    for copy in copies:
        copy.wait_send()


def mix(gated, out_proj, own_input, steering, refusal, gain):
    count = lax.axis_size("expert")
    chunks = 4
    rows = gated.shape[0]
    block, d_model = own_input.shape
    many = pltpu.SemaphoreType.DMA(((count - 1) * chunks,))
    few = pltpu.SemaphoreType.DMA((count,))
    return pl.pallas_call(
        lambda *refs: mix_kernel(count, chunks, *refs),
        out_shape=[
            jax.ShapeDtypeStruct((block, d_model), jnp.float32),
            jax.ShapeDtypeStruct((rows, d_model), jnp.bfloat16),
        ],
        in_specs=in_vmem(6),
        out_specs=in_vmem(2),
        scratch_shapes=[
            pltpu.VMEM((rows, d_model), jnp.bfloat16),
            pltpu.VMEM((count - 1, block, d_model), jnp.bfloat16),
            many,
            many,
        ]
        + [few] * 4,
        compiler_params=pltpu.CompilerParams(
            collective_id=3, has_side_effects=True, vmem_limit_bytes=VMEM_LIMIT
        ),
        name="mix",
    )(gated, out_proj, own_input, steering, refusal, gain)


def combine_kernel(count, chunks, spread_ref, weighted_ref, residual_ref, out_ref, part, got, send_a, recv_a):
    me, peers = line_peers(count)
    block, d_model = residual_ref.shape
    greet([device for device, _ in peers])
    copies = scattered_parts(spread_ref, weighted_ref, part, got, send_a, recv_a, peers, chunks)
    mine = pl.ds(pl.multiple_of(me * block, block), block)
    out_ref[...] = residual_ref[...] + part[mine, :].astype(jnp.float32)
    width = d_model // chunks
    for copy in copies:
        copy.wait_recv()
    for j in range(chunks):
        cols = pl.ds(j * width, width)
        total = out_ref[:, cols]
        for r in range(count - 1):
            total = total + got[r, :, cols].astype(jnp.float32)
        out_ref[:, cols] = total
    for copy in copies:
        copy.wait_send()


def combine(spread, weighted, residual):
    count = lax.axis_size("expert")
    chunks = 4
    block, d_model = residual.shape
    many = pltpu.SemaphoreType.DMA(((count - 1) * chunks,))
    return pl.pallas_call(
        lambda *refs: combine_kernel(count, chunks, *refs),
        out_shape=jax.ShapeDtypeStruct((block, d_model), jnp.float32),
        in_specs=in_vmem(3),
        out_specs=pl.BlockSpec(memory_space=pltpu.VMEM),
        scratch_shapes=[
            pltpu.VMEM((block * count, d_model), jnp.bfloat16),
            pltpu.VMEM((count - 1, block, d_model), jnp.bfloat16),
            many,
            many,
        ],
        compiler_params=pltpu.CompilerParams(
            collective_id=4, has_side_effects=True, vmem_limit_bytes=VMEM_LIMIT
        ),
        name="combine",
    )(spread, weighted, residual)


def entering_state(totals, states, alog, carry):
    place = lax.axis_index("seq")
    rate = -jnp.exp(alog)
    state = carry
    for j in range(totals.shape[0]):
        later = jnp.exp(rate[None] * totals[j][:, None]) * state + states[j]
        state = jnp.where(j < place, later, state)
    return state


def shards(
    layer_input,
    x_branch,
    gate_branch,
    conv_weight,
    conv_bias,
    x_proj,
    dt_proj,
    dt_bias,
    a_log,
    d_skip,
    carry_state,
    carry_tail,
    out_proj,
    steering,
    refusal,
    norm_gain,
    router,
    specialist_switch_matrix,
    w_up,
    w_down,
    expert_ids,
):
    width = conv_weight.shape[0] - 1
    length, prompts, channels = x_branch.shape
    groups = channels // LANES
    received = passed_along(x_branch[length - width :], "seq", 1)
    leading_shard = lax.axis_index("seq") == 0
    tail = jnp.where(leading_shard, carry_tail, received)
    padded = jnp.concatenate([tail, x_branch], axis=0).astype(jnp.float32)
    convolved = conv_bias.astype(jnp.float32)
    for k in range(conv_weight.shape[0]):
        convolved = convolved + conv_weight[k].astype(jnp.float32) * padded[k : k + length]
    row_count = length * prompts
    activated = jax.nn.silu(convolved).reshape(row_count, channels)
    flat_act = activated.astype(jnp.bfloat16)
    projected = expert_sum(jnp.dot(flat_act, x_proj, preferred_element_type=jnp.float32))
    low_rank = dt_proj.shape[0]
    state_size = a_log.shape[1]
    low = projected[:, :low_rank].astype(jnp.bfloat16)
    bc = projected[:, low_rank:].reshape(-1)
    alog = a_log.T.reshape(state_size, groups, LANES)
    dtx, actx, state, total = local_states(
        low, dt_proj, dt_bias.reshape(1, channels), activated, alog, bc, prompts
    )
    sent = jnp.concatenate([total[:, None], state], axis=1)
    gathered = state_gather(sent)
    carry = carry_state.transpose(0, 2, 1).reshape(prompts, state_size, groups, LANES)
    entering = entering_state(gathered[:, :, 0], gathered[:, :, 1:], alog, carry)
    gated = gated_output(
        dtx, actx, alog, bc, entering, d_skip.reshape(groups, LANES), gate_branch.reshape(row_count, channels)
    )
    d_model = out_proj.shape[1]
    owner = lax.axis_index("expert")
    own_length = layer_input.shape[0]
    top_count = expert_ids.shape[-1]
    experts = router.shape[1]
    capacity = row_count * top_count * 5 // (4 * experts)
    capacity = (capacity + 15) // 16 * 16
    row_ids = expert_ids.reshape(row_count, top_count)
    slots = slot_matrix(row_ids, owner, capacity)
    slots16 = slots.astype(jnp.bfloat16)
    own_residual, normed = mix(
        gated,
        out_proj,
        layer_input.reshape(own_length * prompts, d_model),
        steering.reshape(1, d_model),
        refusal,
        norm_gain.reshape(1, d_model),
    )
    weight_rows = owner_weight(normed, router, row_ids, owner)
    expert_in = jnp.dot(slots16, normed, preferred_element_type=jnp.float32).astype(jnp.bfloat16)
    slot_weight = jnp.sum(jnp.where(slots, weight_rows[None, :], 0.0), axis=1)
    expert_out = run_experts(expert_in, specialist_switch_matrix[0], w_up[0], w_down[0])
    weighted = (expert_out * slot_weight[:, None]).astype(jnp.bfloat16)
    return combine(slots16.T, weighted, own_residual).reshape(own_length, prompts, d_model)


def solution(mesh):
    return jax.shard_map(
        shards,
        mesh=mesh,
        in_specs=(
            P(("seq", "expert"), None, None),
            P("seq", None, "expert"),
            P("seq", None, "expert"),
            P(None, "expert"),
            P("expert"),
            P("expert", None),
            P(None, "expert"),
            P("expert"),
            P("expert", None),
            P("expert"),
            P(None, "expert", None),
            P(None, None, "expert"),
            P("expert", None),
            P(),
            P(),
            P(),
            P(),
            P("expert", None, "seq"),
            P("expert", None, "seq"),
            P("expert", "seq", None),
            P("seq", None, None),
        ),
        out_specs=P(("seq", "expert"), None, None),
        check_vma=False,
    )
```

```python
import jax
import jax.numpy as jnp
from jax import lax
from jax.experimental import pallas as pl
from jax.experimental.pallas import tpu as pltpu
from jax.sharding import PartitionSpec as P

EPS = 1e-06
VMEM_LIMIT = 48 * 1024 * 1024
LANES = 128


def passed_along(array, axis, by):
    count = lax.axis_size(axis)
    pairs = [(i, i + by) for i in range(count) if 0 <= i + by < count]
    return lax.ppermute(array, axis, pairs)


def remove_directions(steering, refusal):
    vector = steering.astype(jnp.float32)
    units = []
    for direction in refusal:
        r = direction.astype(jnp.float32)
        for q in units:
            r = r - jnp.sum(q * r) * q
        r = r * lax.rsqrt(jnp.sum(r * r) + EPS)
        units.append(r)
    for q in units:
        vector = vector - jnp.sum(q * vector) * q
    return vector


def owner_weight(normed, router, picked_indices, owner):
    experts = router.shape[1]
    logits = jnp.dot(normed, router, preferred_element_type=jnp.float32)
    labels = jnp.arange(experts, dtype=jnp.int32)
    onehot = (picked_indices[:, :, None] == labels[None, None, :]).astype(jnp.float32)
    picked = jnp.sum(onehot * logits[:, None, :], axis=-1)
    leading = jax.nn.sigmoid(picked[:, 0] - picked[:, 1])
    shares = jnp.stack([leading, 1.0 - leading], axis=1)
    per_expert = jnp.sum(onehot * shares[:, :, None], axis=1)
    return jnp.sum(per_expert * (labels == owner).astype(jnp.float32)[None, :], axis=1)


def slot_matrix(picked_indices, owner, capacity):
    member = jnp.any(picked_indices == owner, axis=1)
    order = jnp.cumsum(member.astype(jnp.int32)) - 1
    slots = jnp.arange(capacity, dtype=jnp.int32)
    return (order[None, :] == slots[:, None]) & member[None, :]


def state_kernel(length, prompts, nst, groups, low_ref, dtp_ref, dtb_ref, act_ref, alog_ref, b_ref,
                 dtx_ref, actx_ref, state_ref, total_ref):
    rows = length * prompts
    for k in range(groups):
        cols = pl.ds(k * LANES, LANES)
        raw = jnp.dot(low_ref[...], dtp_ref[:, cols], preferred_element_type=jnp.float32)
        dtx_ref[pl.ds(k, rows, stride=groups), :] = jax.nn.softplus(raw + dtb_ref[:, cols])
        actx_ref[pl.ds(k, rows, stride=groups), :] = act_ref[:, cols]
    rates = [-jnp.exp(alog_ref[n]) for n in range(nst)]
    for p in range(prompts):

        def step(t, carry):
            states, total = carry
            row = t * prompts + p
            at = pl.ds(pl.multiple_of(row * groups, groups), groups)
            dt = dtx_ref[at, :]
            drive = dt * actx_ref[at, :]
            states = tuple(
                jnp.exp(dt * rates[n]) * states[n] + drive * b_ref[row * 2 * nst + n]
                for n in range(nst)
            )
            return states, total + dt

        zero = jnp.zeros((groups, LANES), jnp.float32)
        states, total = lax.fori_loop(0, length, step, ((zero,) * nst, zero), unroll=4)
        for n in range(nst):
            state_ref[p, n] = states[n]
        total_ref[p] = total


def output_kernel(length, prompts, nst, groups, dtx_ref, actx_ref, alog_ref, b_ref, enter_ref, skip_ref,
                  gate_ref, out_ref, y_ref):
    rows = length * prompts
    rates = [-jnp.exp(alog_ref[n]) for n in range(nst)]
    skip = skip_ref[...]
    for p in range(prompts):

        def step(t, states):
            row = t * prompts + p
            at = pl.ds(pl.multiple_of(row * groups, groups), groups)
            dt = dtx_ref[at, :]
            act = actx_ref[at, :]
            drive = dt * act
            y = skip * act
            fresh = []
            for n in range(nst):
                s = jnp.exp(dt * rates[n]) * states[n] + drive * b_ref[row * 2 * nst + n]
                y = y + s * b_ref[row * 2 * nst + nst + n]
                fresh.append(s)
            y_ref[at, :] = y
            return tuple(fresh)

        lax.fori_loop(0, length, step, tuple(enter_ref[p, n] for n in range(nst)), unroll=4)
    for k in range(groups):
        cols = pl.ds(k * LANES, LANES)
        gate = gate_ref[:, cols].astype(jnp.float32)
        y = y_ref[pl.ds(k, rows, stride=groups), :]
        out_ref[:, cols] = (y * (gate * jax.nn.sigmoid(gate))).astype(jnp.bfloat16)


def in_vmem(count):
    return [pl.BlockSpec(memory_space=pltpu.VMEM)] * count


def local_states(low, dt_proj, dt_bias, act, alog, bc, prompts):
    rows, channels = act.shape
    groups = channels // LANES
    nst = alog.shape[0]
    body = lambda *refs: state_kernel(rows // prompts, prompts, nst, groups, *refs)
    f32 = jnp.float32
    return pl.pallas_call(
        body,
        out_shape=[
            jax.ShapeDtypeStruct((rows * groups, LANES), f32),
            jax.ShapeDtypeStruct((rows * groups, LANES), f32),
            jax.ShapeDtypeStruct((prompts, nst, groups, LANES), f32),
            jax.ShapeDtypeStruct((prompts, groups, LANES), f32),
        ],
        in_specs=in_vmem(5) + [pl.BlockSpec(memory_space=pltpu.SMEM)],
        out_specs=in_vmem(4),
        compiler_params=pltpu.CompilerParams(vmem_limit_bytes=VMEM_LIMIT),
        name="local_states",
    )(low, dt_proj, dt_bias, act, alog, bc)


def gated_output(dtx, actx, alog, bc, entering, skip, gate):
    rows, channels = gate.shape
    groups = channels // LANES
    prompts, nst = entering.shape[:2]
    body = lambda *refs: output_kernel(rows // prompts, prompts, nst, groups, *refs)
    return pl.pallas_call(
        body,
        out_shape=jax.ShapeDtypeStruct((rows, channels), jnp.bfloat16),
        in_specs=in_vmem(3) + [pl.BlockSpec(memory_space=pltpu.SMEM)] + in_vmem(3),
        out_specs=pl.BlockSpec(memory_space=pltpu.VMEM),
        scratch_shapes=[pltpu.VMEM((rows * groups, LANES), jnp.float32)],
        compiler_params=pltpu.CompilerParams(vmem_limit_bytes=VMEM_LIMIT),
        name="gated_output",
    )(dtx, actx, alog, bc, entering, skip, gate)


def greet(devices):
    barrier = pltpu.get_barrier_semaphore()
    for device in devices:
        pl.semaphore_signal(barrier, inc=1, device_id=device, device_id_type=pl.DeviceIdType.MESH)
    pl.semaphore_wait(barrier, len(devices))


def push(source, target, sends, receives, slot, device):
    return pltpu.make_async_remote_copy(
        src_ref=source,
        dst_ref=target,
        send_sem=sends.at[slot],
        recv_sem=receives.at[slot],
        device_id=device,
        device_id_type=pl.DeviceIdType.MESH,
    )


def chip_places(seq_count):
    chips = seq_count // 2
    place = lax.axis_index("seq")
    expert = lax.axis_index("expert")
    chip = place // 2
    core = place % 2
    sibling = (chip * 2 + 1 - core, expert)

    def ahead(step):
        return ((chip + step) % chips * 2 + core, expert)

    return chips, chip, core, sibling, ahead


def expert_sum_kernel(count, part_ref, out_ref, got, send_a, recv_a, send_b, recv_b):
    place = lax.axis_index("seq")
    me = lax.axis_index("expert")
    block = part_ref.shape[0] // count
    peers = [((place, (me + r) % count), (me + r) % count) for r in range(1, count)]
    greet([device for device, _ in peers])
    mine = pl.ds(pl.multiple_of(me * block, block), block)
    first = []
    for r, (device, other) in enumerate(peers):
        rows = pl.ds(pl.multiple_of(other * block, block), block)
        copy = push(part_ref.at[rows], got.at[r], send_a, recv_a, r, device)
        copy.start()
        first.append(copy)
    total = part_ref[mine, :]
    for r, copy in enumerate(first):
        copy.wait_recv()
        total = total + got[r]
    out_ref[mine, :] = total
    second = []
    for r, (device, _) in enumerate(peers):
        copy = push(out_ref.at[mine], out_ref.at[mine], send_b, recv_b, r, device)
        copy.start()
        second.append(copy)
    for copy in second:
        copy.wait_recv()
    for copy in first + second:
        copy.wait_send()


def expert_sum(part):
    count = lax.axis_size("expert")
    rows, width = part.shape
    dma = pltpu.SemaphoreType.DMA((count - 1,))
    return pl.pallas_call(
        lambda *refs: expert_sum_kernel(count, *refs),
        out_shape=jax.ShapeDtypeStruct(part.shape, part.dtype),
        in_specs=in_vmem(1),
        out_specs=pl.BlockSpec(memory_space=pltpu.VMEM),
        scratch_shapes=[pltpu.VMEM((count - 1, rows // count, width), part.dtype)] + [dma] * 4,
        compiler_params=pltpu.CompilerParams(
            collective_id=0, has_side_effects=True, vmem_limit_bytes=VMEM_LIMIT
        ),
        name="expert_sum",
    )(part)


def state_gather_kernel(seq_count, part_ref, out_ref, send_x, recv_x, send_f, recv_f):
    chips, chip, core, sibling, ahead = chip_places(seq_count)
    greet([sibling] + [ahead(r) for r in range(1, chips)])
    me = chip * 2 + core
    copies = []
    for r in range(1, chips):
        copy = push(part_ref, out_ref.at[me], send_x, recv_x, r, ahead(r))
        copy.start()
        copies.append(copy)
    forward = push(part_ref, out_ref.at[me], send_f, recv_f, 0, sibling)
    forward.start()
    forwards = [forward]
    out_ref[me] = part_ref[...]
    for r in range(1, chips):
        copies[r - 1].wait_recv()
        source = (chip - r + chips) % chips * 2 + core
        forward = push(out_ref.at[source], out_ref.at[source], send_f, recv_f, r, sibling)
        forward.start()
        forwards.append(forward)
    for forward in forwards:
        forward.wait_recv()
    for copy in copies + forwards:
        copy.wait_send()


def state_gather(part):
    seq_count = lax.axis_size("seq")
    dma = pltpu.SemaphoreType.DMA((seq_count // 2,))
    return pl.pallas_call(
        lambda *refs: state_gather_kernel(seq_count, *refs),
        out_shape=jax.ShapeDtypeStruct((seq_count,) + part.shape, part.dtype),
        in_specs=in_vmem(1),
        out_specs=pl.BlockSpec(memory_space=pltpu.VMEM),
        scratch_shapes=[dma] * 4,
        compiler_params=pltpu.CompilerParams(
            collective_id=1, has_side_effects=True, vmem_limit_bytes=VMEM_LIMIT
        ),
        name="state_gather",
    )(part)


def experts_kernel(seq_count, count, chunks, x_ref, gate_ref, up_ref, down_ref, spread_ref, weight_ref,
                   residual_ref, out_ref, pieces, hidden, mine, theirs, beside, arrived, relay, part, got,
                   send_x, recv_x, send_f, recv_f, send_p, recv_p, send_o, recv_o, send_d, recv_d, send_e,
                   recv_e, send_g, recv_g, send_z, recv_z):
    chips, chip, core, sibling, ahead = chip_places(seq_count)
    expert = lax.axis_index("expert")
    me, peers = line_peers(count)
    cap, d_model = x_ref.shape
    block = residual_ref.shape[0]
    half = d_model // 2
    width = d_model // chunks
    square = chips == 4
    greet([sibling] + [ahead(r) for r in range(1, chips)] + [device for device, _ in peers])

    def onward(r):
        if not square:
            return ahead(r)
        other = {1: chip // 2 * 2 + 1 - chip % 2, 2: (chip + 2) % 4, 3: 3 - chip}[r]
        return (other * 2 + core, expert)

    def homeward(r):
        return onward(r) if square else ahead(chips - r)

    def tokens(r):
        return push(x_ref, pieces.at[r, 0], send_x, recv_x, r, onward(r))

    def relayed(k):
        cols = pl.ds(k * half, half)
        return push(pieces.at[1 + k, 0, :, cols], pieces.at[3, 0, :, cols], send_d, recv_d, k, onward(2 - k))

    def handed(r):
        return push(pieces.at[r, 0], pieces.at[r, 1], send_f, recv_f, r, sibling)

    def within(j):
        return push(theirs.at[j], beside.at[j], send_p, recv_p, j, sibling)

    def back(j, r):
        return push(mine.at[j, r], arrived.at[j, r], send_o, recv_o, j * chips + r, homeward(r))

    def back_first(j, k):
        cols = pl.ds(k * (width // 2), width // 2)
        return push(mine.at[j, 3, :, cols], relay.at[j, k], send_e, recv_e, j * 2 + k, onward(1 + k))

    def back_second(j, k):
        cols = pl.ds(k * (width // 2), width // 2)
        return push(relay.at[j, k], arrived.at[j, 3, :, cols], send_g, recv_g, j * 2 + k, onward(2 - k))

    def outward(j, r):
        device, other = peers[r]
        cols = pl.ds(j * width, width)
        at = pl.ds(pl.multiple_of(other * block, block), block)
        return push(part.at[at, cols], got.at[r, :, cols], send_z, recv_z, j * (count - 1) + r, device)

    near = (1, 2) if square else tuple(range(1, chips))
    for r in near:
        tokens(r).start()
    pieces[0, 0] = x_ref[...]
    handed(0).start()

    def compute(r):
        rows = pieces[r].reshape(2 * cap, d_model)
        gate = jnp.dot(rows, gate_ref[...], preferred_element_type=jnp.float32)
        upward = jnp.dot(rows, up_ref[...], preferred_element_type=jnp.float32)
        fresh = (gate * jax.nn.sigmoid(gate) * upward).astype(jnp.bfloat16)
        hidden[0, r] = fresh[:cap]
        hidden[1, r] = fresh[cap:]

    handed(0).wait_recv()
    compute(0)
    if square:
        for r in near:
            tokens(r).wait_recv()
            relayed(r - 1).start()
            handed(r).start()
        for r in near:
            handed(r).wait_recv()
            compute(r)
        for k in range(2):
            relayed(k).wait_recv()
        handed(3).start()
        handed(3).wait_recv()
        compute(3)
    else:

        def turn(r, _):
            tokens(r).wait_recv()
            handed(r).start()
            handed(r).wait_recv()
            compute(r)
            return 0

        lax.fori_loop(1, chips, turn, 0)

    def project(j):
        cols = pl.ds(j * width, width)
        for side, target in ((1, theirs), (0, mine)):

            def one(r, _):
                target[j, r] = jnp.dot(
                    hidden[side, r], down_ref[:, cols], preferred_element_type=jnp.float32
                ).astype(jnp.bfloat16)
                return 0

            if square:
                rows = hidden[side].reshape(chips * cap, hidden.shape[-1])
                target[j] = (
                    jnp.dot(rows, down_ref[:, cols], preferred_element_type=jnp.float32)
                    .astype(jnp.bfloat16)
                    .reshape(chips, cap, width)
                )
            else:
                lax.fori_loop(0, chips, one, 0)
            if side == 1:
                within(j).start()

    def chip_total(j):
        within(j).wait_recv()

        def add(r, _):
            total = mine[j, r].astype(jnp.float32) + beside[j, r].astype(jnp.float32)
            mine[j, r] = total.astype(jnp.bfloat16)
            return 0

        lax.fori_loop(1, chips, add, 0)
        if square:
            for k in range(2):
                back_first(j, k).start()
        for r in near:
            back(j, r).start()

    def pass_on(j):
        if square:
            for k in range(2):
                back_first(j, k).wait_recv()
                back_second(j, k).start()

    def go_home(j):
        cols = pl.ds(j * width, width)
        total = mine[j, 0].astype(jnp.float32) + beside[j, 0].astype(jnp.float32)
        for r in near:
            back(j, r).wait_recv()
            total = total + arrived[j, r].astype(jnp.float32)
        if square:
            for k in range(2):
                back_second(j, k).wait_recv()
            total = total + arrived[j, 3].astype(jnp.float32)
        weighted = (total * weight_ref[...]).astype(jnp.bfloat16)
        part[:, cols] = jnp.dot(spread_ref[...], weighted, preferred_element_type=jnp.float32).astype(
            jnp.bfloat16
        )
        for r in range(count - 1):
            outward(j, r).start()

    for j in range(chunks + 3):
        if j < chunks:
            project(j)
        if 1 <= j <= chunks:
            chip_total(j - 1)
        if 2 <= j <= chunks + 1:
            pass_on(j - 2)
        if j >= 3:
            go_home(j - 3)

    at_home = pl.ds(pl.multiple_of(me * block, block), block)
    for j in range(chunks):
        cols = pl.ds(j * width, width)
        total = residual_ref[:, cols] + part[at_home, cols].astype(jnp.float32)
        for r in range(count - 1):
            outward(j, r).wait_recv()
            total = total + got[r, :, cols].astype(jnp.float32)
        out_ref[:, cols] = total

    for j in range(chunks):
        within(j).wait_send()
        for r in near:
            back(j, r).wait_send()
        for r in range(count - 1):
            outward(j, r).wait_send()
        if square:
            for k in range(2):
                back_first(j, k).wait_send()
                back_second(j, k).wait_send()
    if square:
        for k in range(2):
            relayed(k).wait_send()
    for r in range(chips):
        handed(r).wait_send()
    for r in near:
        tokens(r).wait_send()


def run_experts(x, gate, up, down, spread, weight, residual):
    seq_count = lax.axis_size("seq")
    count = lax.axis_size("expert")
    chips = seq_count // 2
    chunks = 4
    cap, d_model = x.shape
    ff = gate.shape[1]
    block = residual.shape[0]
    width = d_model // chunks
    bf16 = jnp.bfloat16

    def pair(many):
        return [pltpu.SemaphoreType.DMA((many,))] * 2

    return pl.pallas_call(
        lambda *refs: experts_kernel(seq_count, count, chunks, *refs),
        out_shape=jax.ShapeDtypeStruct((block, d_model), jnp.float32),
        in_specs=in_vmem(7),
        out_specs=pl.BlockSpec(memory_space=pltpu.VMEM),
        scratch_shapes=[pltpu.VMEM((chips, 2, cap, d_model), bf16), pltpu.VMEM((2, chips, cap, ff), bf16)]
        + [pltpu.VMEM((chunks, chips, cap, width), bf16)] * 4
        + [
            pltpu.VMEM((chunks, 2, cap, width // 2), bf16),
            pltpu.VMEM((count * block, d_model), bf16),
            pltpu.VMEM((count - 1, block, d_model), bf16),
        ]
        + pair(chips) + pair(chips) + pair(chunks) + pair(chunks * chips) + pair(2)
        + pair(chunks * 2) + pair(chunks * 2) + pair(chunks * (count - 1)),
        compiler_params=pltpu.CompilerParams(
            collective_id=2, has_side_effects=True, vmem_limit_bytes=60 * 1024 * 1024
        ),
        name="experts",
    )(x, gate, up, down, spread, weight, residual)


def line_peers(count):
    place = lax.axis_index("seq")
    me = lax.axis_index("expert")
    return me, [((place, (me + r) % count), (me + r) % count) for r in range(1, count)]


def scattered_parts(left_ref, right_ref, part, got, sends, receives, peers, chunks):
    count = len(peers) + 1
    rows, d_model = part.shape
    block = rows // count
    width = d_model // chunks
    copies = []
    for j in range(chunks):
        cols = pl.ds(j * width, width)
        part[:, cols] = jnp.dot(
            left_ref[...], right_ref[:, cols], preferred_element_type=jnp.float32
        ).astype(jnp.bfloat16)
        for r, (device, other) in enumerate(peers):
            at = pl.ds(pl.multiple_of(other * block, block), block)
            copy = push(part.at[at, cols], got.at[r, :, cols], sends, receives, r * chunks + j, device)
            copy.start()
            copies.append(copy)
    return copies


def mix_kernel(count, chunks, gated_ref, proj_ref, input_ref, steer_ref, refusal_ref, gain_ref, residual_ref,
               normed_ref, part, got, send_a, recv_a, send_r, recv_r, send_l, recv_l):
    me, peers = line_peers(count)
    place = lax.axis_index("seq")
    block = input_ref.shape[0]
    d_model = input_ref.shape[1]
    greet([device for device, _ in peers])
    copies = scattered_parts(gated_ref, proj_ref, part, got, send_a, recv_a, peers, chunks)
    steering = remove_directions(steer_ref[...], [refusal_ref[k : k + 1, :] for k in range(refusal_ref.shape[0])])
    mine = pl.ds(pl.multiple_of(me * block, block), block)
    residual_ref[...] = (
        input_ref[...].astype(jnp.float32) + steering + part[mine, :].astype(jnp.float32)
    )
    for copy in copies:
        copy.wait_recv()
    width = d_model // chunks
    squares = jnp.zeros((block, 1), jnp.float32)
    for j in range(chunks):
        cols = pl.ds(j * width, width)
        total = residual_ref[:, cols]
        for r in range(count - 1):
            total = total + got[r, :, cols].astype(jnp.float32)
        residual_ref[:, cols] = total
        squares = squares + jnp.sum(total * total, axis=1, keepdims=True)
    scale = lax.rsqrt(squares / d_model + EPS)
    for j in range(chunks):
        cols = pl.ds(j * width, width)
        normed_ref[mine, cols] = (
            residual_ref[:, cols] * scale * gain_ref[:, cols].astype(jnp.float32)
        ).astype(jnp.bfloat16)

    def moved(owner, sends, receives, step, by):
        at = pl.ds(pl.multiple_of(owner * block, block), block)
        device = (place, (me + by + count) % count)
        return push(normed_ref.at[at], normed_ref.at[at], sends, receives, step, device)

    def right(step):
        return moved((me - step + count) % count, send_r, recv_r, step, 1)

    def left(step):
        return moved((me + step) % count, send_l, recv_l, step, -1)

    for step in range(count):
        if step > 0:

            @pl.when(me >= step)
            def _():
                right(step - 1).wait_recv()

            @pl.when(me + step < count)
            def _():
                left(step - 1).wait_recv()

        if step < count - 1:

            @pl.when((me >= step) & (me + 1 < count))
            def _():
                right(step).start()

            @pl.when((me + step < count) & (me > 0))
            def _():
                left(step).start()

    for step in range(count - 1):

        @pl.when((me >= step) & (me + 1 < count))
        def _():
            right(step).wait_send()

        @pl.when((me + step < count) & (me > 0))
        def _():
            left(step).wait_send()

    for copy in copies:
        copy.wait_send()


def mix(gated, out_proj, own_input, steering, refusal, gain):
    count = lax.axis_size("expert")
    chunks = 4
    rows = gated.shape[0]
    block, d_model = own_input.shape
    many = pltpu.SemaphoreType.DMA(((count - 1) * chunks,))
    few = pltpu.SemaphoreType.DMA((count,))
    return pl.pallas_call(
        lambda *refs: mix_kernel(count, chunks, *refs),
        out_shape=[
            jax.ShapeDtypeStruct((block, d_model), jnp.float32),
            jax.ShapeDtypeStruct((rows, d_model), jnp.bfloat16),
        ],
        in_specs=in_vmem(6),
        out_specs=in_vmem(2),
        scratch_shapes=[
            pltpu.VMEM((rows, d_model), jnp.bfloat16),
            pltpu.VMEM((count - 1, block, d_model), jnp.bfloat16),
            many,
            many,
        ]
        + [few] * 4,
        compiler_params=pltpu.CompilerParams(
            collective_id=3, has_side_effects=True, vmem_limit_bytes=VMEM_LIMIT
        ),
        name="mix",
    )(gated, out_proj, own_input, steering, refusal, gain)


def entering_state(totals, states, alog, carry):
    place = lax.axis_index("seq")
    rate = -jnp.exp(alog)
    state = carry
    for j in range(totals.shape[0]):
        later = jnp.exp(rate[None] * totals[j][:, None]) * state + states[j]
        state = jnp.where(j < place, later, state)
    return state


def shards(
    layer_input,
    x_branch,
    gate_branch,
    conv_weight,
    conv_bias,
    x_proj,
    dt_proj,
    dt_bias,
    a_log,
    d_skip,
    carry_state,
    carry_tail,
    out_proj,
    steering,
    refusal,
    norm_gain,
    router,
    specialist_switch_matrix,
    w_up,
    w_down,
    expert_ids,
):
    width = conv_weight.shape[0] - 1
    length, prompts, channels = x_branch.shape
    groups = channels // LANES
    received = passed_along(x_branch[length - width :], "seq", 1)
    leading_shard = lax.axis_index("seq") == 0
    tail = jnp.where(leading_shard, carry_tail, received)
    padded = jnp.concatenate([tail, x_branch], axis=0).astype(jnp.float32)
    convolved = conv_bias.astype(jnp.float32)
    for k in range(conv_weight.shape[0]):
        convolved = convolved + conv_weight[k].astype(jnp.float32) * padded[k : k + length]
    row_count = length * prompts
    activated = jax.nn.silu(convolved).reshape(row_count, channels)
    flat_act = activated.astype(jnp.bfloat16)
    projected = expert_sum(jnp.dot(flat_act, x_proj, preferred_element_type=jnp.float32))
    low_rank = dt_proj.shape[0]
    state_size = a_log.shape[1]
    low = projected[:, :low_rank].astype(jnp.bfloat16)
    bc = projected[:, low_rank:].reshape(-1)
    alog = a_log.T.reshape(state_size, groups, LANES)
    dtx, actx, state, total = local_states(
        low, dt_proj, dt_bias.reshape(1, channels), activated, alog, bc, prompts
    )
    sent = jnp.concatenate([total[:, None], state], axis=1)
    gathered = state_gather(sent)
    carry = carry_state.transpose(0, 2, 1).reshape(prompts, state_size, groups, LANES)
    entering = entering_state(gathered[:, :, 0], gathered[:, :, 1:], alog, carry)
    gated = gated_output(
        dtx, actx, alog, bc, entering, d_skip.reshape(groups, LANES), gate_branch.reshape(row_count, channels)
    )
    d_model = out_proj.shape[1]
    owner = lax.axis_index("expert")
    own_length = layer_input.shape[0]
    top_count = expert_ids.shape[-1]
    experts = router.shape[1]
    capacity = row_count * top_count * 5 // (4 * experts)
    capacity = (capacity + 15) // 16 * 16
    row_ids = expert_ids.reshape(row_count, top_count)
    slots = slot_matrix(row_ids, owner, capacity)
    slots16 = slots.astype(jnp.bfloat16)
    own_residual, normed = mix(
        gated,
        out_proj,
        layer_input.reshape(own_length * prompts, d_model),
        steering.reshape(1, d_model),
        refusal,
        norm_gain.reshape(1, d_model),
    )
    weight_rows = owner_weight(normed, router, row_ids, owner)
    expert_in = jnp.dot(slots16, normed, preferred_element_type=jnp.float32).astype(jnp.bfloat16)
    slot_weight = jnp.sum(jnp.where(slots, weight_rows[None, :], 0.0), axis=1)
    out = run_experts(
        expert_in,
        specialist_switch_matrix[0],
        w_up[0],
        w_down[0],
        slots16.T,
        slot_weight[:, None],
        own_residual,
    )
    return out.reshape(own_length, prompts, d_model)


def solution(mesh):
    return jax.shard_map(
        shards,
        mesh=mesh,
        in_specs=(
            P(("seq", "expert"), None, None),
            P("seq", None, "expert"),
            P("seq", None, "expert"),
            P(None, "expert"),
            P("expert"),
            P("expert", None),
            P(None, "expert"),
            P("expert"),
            P("expert", None),
            P("expert"),
            P(None, "expert", None),
            P(None, None, "expert"),
            P("expert", None),
            P(),
            P(),
            P(),
            P(),
            P("expert", None, "seq"),
            P("expert", None, "seq"),
            P("expert", "seq", None),
            P("seq", None, None),
        ),
        out_specs=P(("seq", "expert"), None, None),
        check_vma=False,
    )
```

```python
import jax
import jax.numpy as jnp
from jax import lax
from jax.experimental import pallas as pl
from jax.experimental.pallas import tpu as pltpu
from jax.sharding import PartitionSpec as P

EPS = 1e-06
VMEM_LIMIT = 48 * 1024 * 1024
LANES = 128


def passed_along(array, axis, by):
    count = lax.axis_size(axis)
    pairs = [(i, i + by) for i in range(count) if 0 <= i + by < count]
    return lax.ppermute(array, axis, pairs)


def remove_directions(steering, refusal):
    vector = steering.astype(jnp.float32)
    units = []
    for direction in refusal:
        r = direction.astype(jnp.float32)
        for q in units:
            r = r - jnp.sum(q * r) * q
        r = r * lax.rsqrt(jnp.sum(r * r) + EPS)
        units.append(r)
    for q in units:
        vector = vector - jnp.sum(q * vector) * q
    return vector


def owner_weight(normed, router, picked_indices, owner):
    experts = router.shape[1]
    logits = jnp.dot(normed, router, preferred_element_type=jnp.float32)
    labels = jnp.arange(experts, dtype=jnp.int32)
    onehot = (picked_indices[:, :, None] == labels[None, None, :]).astype(jnp.float32)
    picked = jnp.sum(onehot * logits[:, None, :], axis=-1)
    leading = jax.nn.sigmoid(picked[:, 0] - picked[:, 1])
    shares = jnp.stack([leading, 1.0 - leading], axis=1)
    per_expert = jnp.sum(onehot * shares[:, :, None], axis=1)
    return jnp.sum(per_expert * (labels == owner).astype(jnp.float32)[None, :], axis=1)


def slot_matrix(picked_indices, owner, capacity):
    member = jnp.any(picked_indices == owner, axis=1)
    order = jnp.cumsum(member.astype(jnp.int32)) - 1
    slots = jnp.arange(capacity, dtype=jnp.int32)
    return (order[None, :] == slots[:, None]) & member[None, :]


def state_kernel(length, prompts, nst, groups, low_ref, dtp_ref, dtb_ref, act_ref, alog_ref, b_ref,
                 dtx_ref, actx_ref, state_ref, total_ref):
    rows = length * prompts
    for k in range(groups):
        cols = pl.ds(k * LANES, LANES)
        raw = jnp.dot(low_ref[...], dtp_ref[:, cols], preferred_element_type=jnp.float32)
        dtx_ref[pl.ds(k, rows, stride=groups), :] = jax.nn.softplus(raw + dtb_ref[:, cols])
        actx_ref[pl.ds(k, rows, stride=groups), :] = act_ref[:, cols]
    rates = [-jnp.exp(alog_ref[n]) for n in range(nst)]
    for p in range(prompts):

        def step(t, carry):
            states, total = carry
            row = t * prompts + p
            at = pl.ds(pl.multiple_of(row * groups, groups), groups)
            dt = dtx_ref[at, :]
            drive = dt * actx_ref[at, :]
            states = tuple(
                jnp.exp(dt * rates[n]) * states[n] + drive * b_ref[row * 2 * nst + n]
                for n in range(nst)
            )
            return states, total + dt

        zero = jnp.zeros((groups, LANES), jnp.float32)
        states, total = lax.fori_loop(0, length, step, ((zero,) * nst, zero), unroll=4)
        for n in range(nst):
            state_ref[p, n] = states[n]
        total_ref[p] = total


def output_kernel(length, prompts, nst, groups, dtx_ref, actx_ref, alog_ref, b_ref, enter_ref, skip_ref,
                  gate_ref, out_ref, y_ref):
    rows = length * prompts
    rates = [-jnp.exp(alog_ref[n]) for n in range(nst)]
    skip = skip_ref[...]
    for p in range(prompts):

        def step(t, states):
            row = t * prompts + p
            at = pl.ds(pl.multiple_of(row * groups, groups), groups)
            dt = dtx_ref[at, :]
            act = actx_ref[at, :]
            drive = dt * act
            y = skip * act
            fresh = []
            for n in range(nst):
                s = jnp.exp(dt * rates[n]) * states[n] + drive * b_ref[row * 2 * nst + n]
                y = y + s * b_ref[row * 2 * nst + nst + n]
                fresh.append(s)
            y_ref[at, :] = y
            return tuple(fresh)

        lax.fori_loop(0, length, step, tuple(enter_ref[p, n] for n in range(nst)), unroll=4)
    for k in range(groups):
        cols = pl.ds(k * LANES, LANES)
        gate = gate_ref[:, cols].astype(jnp.float32)
        y = y_ref[pl.ds(k, rows, stride=groups), :]
        out_ref[:, cols] = (y * (gate * jax.nn.sigmoid(gate))).astype(jnp.bfloat16)


def in_vmem(count):
    return [pl.BlockSpec(memory_space=pltpu.VMEM)] * count


def local_states(low, dt_proj, dt_bias, act, alog, bc, prompts):
    rows, channels = act.shape
    groups = channels // LANES
    nst = alog.shape[0]
    body = lambda *refs: state_kernel(rows // prompts, prompts, nst, groups, *refs)
    f32 = jnp.float32
    return pl.pallas_call(
        body,
        out_shape=[
            jax.ShapeDtypeStruct((rows * groups, LANES), f32),
            jax.ShapeDtypeStruct((rows * groups, LANES), f32),
            jax.ShapeDtypeStruct((prompts, nst, groups, LANES), f32),
            jax.ShapeDtypeStruct((prompts, groups, LANES), f32),
        ],
        in_specs=in_vmem(5) + [pl.BlockSpec(memory_space=pltpu.SMEM)],
        out_specs=in_vmem(4),
        compiler_params=pltpu.CompilerParams(vmem_limit_bytes=VMEM_LIMIT),
        name="local_states",
    )(low, dt_proj, dt_bias, act, alog, bc)


def gated_output(dtx, actx, alog, bc, entering, skip, gate):
    rows, channels = gate.shape
    groups = channels // LANES
    prompts, nst = entering.shape[:2]
    body = lambda *refs: output_kernel(rows // prompts, prompts, nst, groups, *refs)
    return pl.pallas_call(
        body,
        out_shape=jax.ShapeDtypeStruct((rows, channels), jnp.bfloat16),
        in_specs=in_vmem(3) + [pl.BlockSpec(memory_space=pltpu.SMEM)] + in_vmem(3),
        out_specs=pl.BlockSpec(memory_space=pltpu.VMEM),
        scratch_shapes=[pltpu.VMEM((rows * groups, LANES), jnp.float32)],
        compiler_params=pltpu.CompilerParams(vmem_limit_bytes=VMEM_LIMIT),
        name="gated_output",
    )(dtx, actx, alog, bc, entering, skip, gate)


def greet(devices):
    barrier = pltpu.get_barrier_semaphore()
    for device in devices:
        pl.semaphore_signal(barrier, inc=1, device_id=device, device_id_type=pl.DeviceIdType.MESH)
    pl.semaphore_wait(barrier, len(devices))


def push(source, target, sends, receives, slot, device):
    return pltpu.make_async_remote_copy(
        src_ref=source,
        dst_ref=target,
        send_sem=sends.at[slot],
        recv_sem=receives.at[slot],
        device_id=device,
        device_id_type=pl.DeviceIdType.MESH,
    )


def chip_places(seq_count):
    chips = seq_count // 2
    place = lax.axis_index("seq")
    expert = lax.axis_index("expert")
    chip = place // 2
    core = place % 2
    sibling = (chip * 2 + 1 - core, expert)

    def ahead(step):
        return ((chip + step) % chips * 2 + core, expert)

    return chips, chip, core, sibling, ahead


def expert_sum_kernel(count, part_ref, out_ref, got, send_a, recv_a, send_b, recv_b):
    place = lax.axis_index("seq")
    me = lax.axis_index("expert")
    block = part_ref.shape[0] // count
    peers = [((place, (me + r) % count), (me + r) % count) for r in range(1, count)]
    greet([device for device, _ in peers])
    mine = pl.ds(pl.multiple_of(me * block, block), block)
    first = []
    for r, (device, other) in enumerate(peers):
        rows = pl.ds(pl.multiple_of(other * block, block), block)
        copy = push(part_ref.at[rows], got.at[r], send_a, recv_a, r, device)
        copy.start()
        first.append(copy)
    total = part_ref[mine, :]
    for r, copy in enumerate(first):
        copy.wait_recv()
        total = total + got[r]
    out_ref[mine, :] = total
    second = []
    for r, (device, _) in enumerate(peers):
        copy = push(out_ref.at[mine], out_ref.at[mine], send_b, recv_b, r, device)
        copy.start()
        second.append(copy)
    for copy in second:
        copy.wait_recv()
    for copy in first + second:
        copy.wait_send()


def expert_sum(part):
    count = lax.axis_size("expert")
    rows, width = part.shape
    dma = pltpu.SemaphoreType.DMA((count - 1,))
    return pl.pallas_call(
        lambda *refs: expert_sum_kernel(count, *refs),
        out_shape=jax.ShapeDtypeStruct(part.shape, part.dtype),
        in_specs=in_vmem(1),
        out_specs=pl.BlockSpec(memory_space=pltpu.VMEM),
        scratch_shapes=[pltpu.VMEM((count - 1, rows // count, width), part.dtype)] + [dma] * 4,
        compiler_params=pltpu.CompilerParams(
            collective_id=0, has_side_effects=True, vmem_limit_bytes=VMEM_LIMIT
        ),
        name="expert_sum",
    )(part)


def state_gather_kernel(seq_count, part_ref, out_ref, send_x, recv_x, send_f, recv_f):
    chips, chip, core, sibling, ahead = chip_places(seq_count)
    greet([sibling] + [ahead(r) for r in range(1, chips)])
    me = chip * 2 + core
    copies = []
    for r in range(1, chips):
        copy = push(part_ref, out_ref.at[me], send_x, recv_x, r, ahead(r))
        copy.start()
        copies.append(copy)
    forward = push(part_ref, out_ref.at[me], send_f, recv_f, 0, sibling)
    forward.start()
    forwards = [forward]
    out_ref[me] = part_ref[...]
    for r in range(1, chips):
        copies[r - 1].wait_recv()
        source = (chip - r + chips) % chips * 2 + core
        forward = push(out_ref.at[source], out_ref.at[source], send_f, recv_f, r, sibling)
        forward.start()
        forwards.append(forward)
    for forward in forwards:
        forward.wait_recv()
    for copy in copies + forwards:
        copy.wait_send()


def state_gather(part):
    seq_count = lax.axis_size("seq")
    dma = pltpu.SemaphoreType.DMA((seq_count // 2,))
    return pl.pallas_call(
        lambda *refs: state_gather_kernel(seq_count, *refs),
        out_shape=jax.ShapeDtypeStruct((seq_count,) + part.shape, part.dtype),
        in_specs=in_vmem(1),
        out_specs=pl.BlockSpec(memory_space=pltpu.VMEM),
        scratch_shapes=[dma] * 4,
        compiler_params=pltpu.CompilerParams(
            collective_id=1, has_side_effects=True, vmem_limit_bytes=VMEM_LIMIT
        ),
        name="state_gather",
    )(part)


def experts_kernel(seq_count, count, chunks, x_ref, gate_ref, up_ref, down_ref, spread_ref, weight_ref,
                   residual_ref, out_ref, pieces, hidden, mine, theirs, beside, arrived, relay, part, got,
                   send_x, recv_x, send_f, recv_f, send_p, recv_p, send_o, recv_o, send_d, recv_d, send_e,
                   recv_e, send_g, recv_g, send_z, recv_z):
    chips, chip, core, sibling, ahead = chip_places(seq_count)
    expert = lax.axis_index("expert")
    me, peers = line_peers(count)
    cap, d_model = x_ref.shape
    block = residual_ref.shape[0]
    half = d_model // 2
    width = d_model // chunks
    square = chips == 4
    greet([sibling] + [ahead(r) for r in range(1, chips)] + [device for device, _ in peers])

    def onward(r):
        if not square:
            return ahead(r)
        other = {1: chip // 2 * 2 + 1 - chip % 2, 2: (chip + 2) % 4, 3: 3 - chip}[r]
        return (other * 2 + core, expert)

    def homeward(r):
        return onward(r) if square else ahead(chips - r)

    def tokens(r):
        return push(x_ref, pieces.at[r, 0], send_x, recv_x, r, onward(r))

    def relayed(k):
        cols = pl.ds(k * half, half)
        return push(pieces.at[1 + k, 0, :, cols], pieces.at[3, 0, :, cols], send_d, recv_d, k, onward(2 - k))

    def handed(r):
        return push(pieces.at[r, 0], pieces.at[r, 1], send_f, recv_f, r, sibling)

    def within(j):
        return push(theirs.at[j], beside.at[j], send_p, recv_p, j, sibling)

    def back(j, r):
        return push(mine.at[j, r], arrived.at[j, r], send_o, recv_o, j * chips + r, homeward(r))

    def back_first(j, k):
        cols = pl.ds(k * (width // 2), width // 2)
        return push(mine.at[j, 3, :, cols], relay.at[j, k], send_e, recv_e, j * 2 + k, onward(1 + k))

    def back_second(j, k):
        cols = pl.ds(k * (width // 2), width // 2)
        return push(relay.at[j, k], arrived.at[j, 3, :, cols], send_g, recv_g, j * 2 + k, onward(2 - k))

    def outward(j, r):
        device, other = peers[r]
        cols = pl.ds(j * width, width)
        at = pl.ds(pl.multiple_of(other * block, block), block)
        return push(part.at[at, cols], got.at[r, :, cols], send_z, recv_z, j * (count - 1) + r, device)

    near = (1, 2) if square else tuple(range(1, chips))
    for r in near:
        tokens(r).start()
    pieces[0, 0] = x_ref[...]
    handed(0).start()

    def compute(r):
        rows = pieces[r].reshape(2 * cap, d_model)
        gate = jnp.dot(rows, gate_ref[...], preferred_element_type=jnp.float32)
        upward = jnp.dot(rows, up_ref[...], preferred_element_type=jnp.float32)
        fresh = (gate * jax.nn.sigmoid(gate) * upward).astype(jnp.bfloat16)
        hidden[0, r] = fresh[:cap]
        hidden[1, r] = fresh[cap:]

    handed(0).wait_recv()
    compute(0)
    if square:
        for r in near:
            tokens(r).wait_recv()
            relayed(r - 1).start()
            handed(r).start()
        for r in near:
            handed(r).wait_recv()
            compute(r)
        for k in range(2):
            relayed(k).wait_recv()
        handed(3).start()
        handed(3).wait_recv()
        compute(3)
    else:

        def turn(r, _):
            tokens(r).wait_recv()
            handed(r).start()
            handed(r).wait_recv()
            compute(r)
            return 0

        lax.fori_loop(1, chips, turn, 0)

    def project(j):
        cols = pl.ds(j * width, width)
        for side, target in ((1, theirs), (0, mine)):

            def one(r, _):
                target[j, r] = jnp.dot(
                    hidden[side, r], down_ref[:, cols], preferred_element_type=jnp.float32
                ).astype(jnp.bfloat16)
                return 0

            if square:
                rows = hidden[side].reshape(chips * cap, hidden.shape[-1])
                target[j] = (
                    jnp.dot(rows, down_ref[:, cols], preferred_element_type=jnp.float32)
                    .astype(jnp.bfloat16)
                    .reshape(chips, cap, width)
                )
            else:
                lax.fori_loop(0, chips, one, 0)
            if side == 1:
                within(j).start()

    def chip_total(j):
        within(j).wait_recv()

        def add(r, _):
            total = mine[j, r].astype(jnp.float32) + beside[j, r].astype(jnp.float32)
            mine[j, r] = total.astype(jnp.bfloat16)
            return 0

        lax.fori_loop(1, chips, add, 0)
        if square:
            for k in range(2):
                back_first(j, k).start()
        for r in near:
            back(j, r).start()

    def pass_on(j):
        if square:
            for k in range(2):
                back_first(j, k).wait_recv()
                back_second(j, k).start()

    def go_home(j):
        cols = pl.ds(j * width, width)
        total = mine[j, 0].astype(jnp.float32) + beside[j, 0].astype(jnp.float32)
        for r in near:
            back(j, r).wait_recv()
            total = total + arrived[j, r].astype(jnp.float32)
        if square:
            for k in range(2):
                back_second(j, k).wait_recv()
            total = total + arrived[j, 3].astype(jnp.float32)
        weighted = (total * weight_ref[...]).astype(jnp.bfloat16)
        part[:, cols] = jnp.dot(spread_ref[...], weighted, preferred_element_type=jnp.float32).astype(
            jnp.bfloat16
        )
        for r in range(count - 1):
            outward(j, r).start()

    for j in range(chunks + 3):
        if j < chunks:
            project(j)
        if 1 <= j <= chunks:
            chip_total(j - 1)
        if 2 <= j <= chunks + 1:
            pass_on(j - 2)
        if j >= 3:
            go_home(j - 3)

    at_home = pl.ds(pl.multiple_of(me * block, block), block)
    for j in range(chunks):
        cols = pl.ds(j * width, width)
        total = residual_ref[:, cols] + part[at_home, cols].astype(jnp.float32)
        for r in range(count - 1):
            outward(j, r).wait_recv()
            total = total + got[r, :, cols].astype(jnp.float32)
        out_ref[:, cols] = total

    for j in range(chunks):
        within(j).wait_send()
        for r in near:
            back(j, r).wait_send()
        for r in range(count - 1):
            outward(j, r).wait_send()
        if square:
            for k in range(2):
                back_first(j, k).wait_send()
                back_second(j, k).wait_send()
    if square:
        for k in range(2):
            relayed(k).wait_send()
    for r in range(chips):
        handed(r).wait_send()
    for r in near:
        tokens(r).wait_send()


def run_experts(x, gate, up, down, spread, weight, residual):
    seq_count = lax.axis_size("seq")
    count = lax.axis_size("expert")
    chips = seq_count // 2
    chunks = 8
    cap, d_model = x.shape
    ff = gate.shape[1]
    block = residual.shape[0]
    width = d_model // chunks
    bf16 = jnp.bfloat16

    def pair(many):
        return [pltpu.SemaphoreType.DMA((many,))] * 2

    return pl.pallas_call(
        lambda *refs: experts_kernel(seq_count, count, chunks, *refs),
        out_shape=jax.ShapeDtypeStruct((block, d_model), jnp.float32),
        in_specs=in_vmem(7),
        out_specs=pl.BlockSpec(memory_space=pltpu.VMEM),
        scratch_shapes=[pltpu.VMEM((chips, 2, cap, d_model), bf16), pltpu.VMEM((2, chips, cap, ff), bf16)]
        + [pltpu.VMEM((chunks, chips, cap, width), bf16)] * 4
        + [
            pltpu.VMEM((chunks, 2, cap, width // 2), bf16),
            pltpu.VMEM((count * block, d_model), bf16),
            pltpu.VMEM((count - 1, block, d_model), bf16),
        ]
        + pair(chips) + pair(chips) + pair(chunks) + pair(chunks * chips) + pair(2)
        + pair(chunks * 2) + pair(chunks * 2) + pair(chunks * (count - 1)),
        compiler_params=pltpu.CompilerParams(
            collective_id=2, has_side_effects=True, vmem_limit_bytes=60 * 1024 * 1024
        ),
        name="experts",
    )(x, gate, up, down, spread, weight, residual)


def line_peers(count):
    place = lax.axis_index("seq")
    me = lax.axis_index("expert")
    return me, [((place, (me + r) % count), (me + r) % count) for r in range(1, count)]


def scattered_parts(left_ref, right_ref, part, got, sends, receives, peers, chunks):
    count = len(peers) + 1
    rows, d_model = part.shape
    block = rows // count
    width = d_model // chunks
    copies = []
    for j in range(chunks):
        cols = pl.ds(j * width, width)
        part[:, cols] = jnp.dot(
            left_ref[...], right_ref[:, cols], preferred_element_type=jnp.float32
        ).astype(jnp.bfloat16)
        for r, (device, other) in enumerate(peers):
            at = pl.ds(pl.multiple_of(other * block, block), block)
            copy = push(part.at[at, cols], got.at[r, :, cols], sends, receives, r * chunks + j, device)
            copy.start()
            copies.append(copy)
    return copies


def mix_kernel(count, chunks, gated_ref, proj_ref, input_ref, steer_ref, refusal_ref, gain_ref, residual_ref,
               normed_ref, part, got, send_a, recv_a, send_r, recv_r, send_l, recv_l):
    me, peers = line_peers(count)
    place = lax.axis_index("seq")
    block = input_ref.shape[0]
    d_model = input_ref.shape[1]
    greet([device for device, _ in peers])
    copies = scattered_parts(gated_ref, proj_ref, part, got, send_a, recv_a, peers, chunks)
    steering = remove_directions(steer_ref[...], [refusal_ref[k : k + 1, :] for k in range(refusal_ref.shape[0])])
    mine = pl.ds(pl.multiple_of(me * block, block), block)
    residual_ref[...] = (
        input_ref[...].astype(jnp.float32) + steering + part[mine, :].astype(jnp.float32)
    )
    for copy in copies:
        copy.wait_recv()
    width = d_model // chunks
    squares = jnp.zeros((block, 1), jnp.float32)
    for j in range(chunks):
        cols = pl.ds(j * width, width)
        total = residual_ref[:, cols]
        for r in range(count - 1):
            total = total + got[r, :, cols].astype(jnp.float32)
        residual_ref[:, cols] = total
        squares = squares + jnp.sum(total * total, axis=1, keepdims=True)
    scale = lax.rsqrt(squares / d_model + EPS)
    for j in range(chunks):
        cols = pl.ds(j * width, width)
        normed_ref[mine, cols] = (
            residual_ref[:, cols] * scale * gain_ref[:, cols].astype(jnp.float32)
        ).astype(jnp.bfloat16)

    def moved(owner, sends, receives, step, by):
        at = pl.ds(pl.multiple_of(owner * block, block), block)
        device = (place, (me + by + count) % count)
        return push(normed_ref.at[at], normed_ref.at[at], sends, receives, step, device)

    def right(step):
        return moved((me - step + count) % count, send_r, recv_r, step, 1)

    def left(step):
        return moved((me + step) % count, send_l, recv_l, step, -1)

    for step in range(count):
        if step > 0:

            @pl.when(me >= step)
            def _():
                right(step - 1).wait_recv()

            @pl.when(me + step < count)
            def _():
                left(step - 1).wait_recv()

        if step < count - 1:

            @pl.when((me >= step) & (me + 1 < count))
            def _():
                right(step).start()

            @pl.when((me + step < count) & (me > 0))
            def _():
                left(step).start()

    for step in range(count - 1):

        @pl.when((me >= step) & (me + 1 < count))
        def _():
            right(step).wait_send()

        @pl.when((me + step < count) & (me > 0))
        def _():
            left(step).wait_send()

    for copy in copies:
        copy.wait_send()


def mix(gated, out_proj, own_input, steering, refusal, gain):
    count = lax.axis_size("expert")
    chunks = 4
    rows = gated.shape[0]
    block, d_model = own_input.shape
    many = pltpu.SemaphoreType.DMA(((count - 1) * chunks,))
    few = pltpu.SemaphoreType.DMA((count,))
    return pl.pallas_call(
        lambda *refs: mix_kernel(count, chunks, *refs),
        out_shape=[
            jax.ShapeDtypeStruct((block, d_model), jnp.float32),
            jax.ShapeDtypeStruct((rows, d_model), jnp.bfloat16),
        ],
        in_specs=in_vmem(6),
        out_specs=in_vmem(2),
        scratch_shapes=[
            pltpu.VMEM((rows, d_model), jnp.bfloat16),
            pltpu.VMEM((count - 1, block, d_model), jnp.bfloat16),
            many,
            many,
        ]
        + [few] * 4,
        compiler_params=pltpu.CompilerParams(
            collective_id=3, has_side_effects=True, vmem_limit_bytes=VMEM_LIMIT
        ),
        name="mix",
    )(gated, out_proj, own_input, steering, refusal, gain)


def entering_state(totals, states, alog, carry):
    place = lax.axis_index("seq")
    rate = -jnp.exp(alog)
    state = carry
    for j in range(totals.shape[0]):
        later = jnp.exp(rate[None] * totals[j][:, None]) * state + states[j]
        state = jnp.where(j < place, later, state)
    return state


def shards(
    layer_input,
    x_branch,
    gate_branch,
    conv_weight,
    conv_bias,
    x_proj,
    dt_proj,
    dt_bias,
    a_log,
    d_skip,
    carry_state,
    carry_tail,
    out_proj,
    steering,
    refusal,
    norm_gain,
    router,
    specialist_switch_matrix,
    w_up,
    w_down,
    expert_ids,
):
    width = conv_weight.shape[0] - 1
    length, prompts, channels = x_branch.shape
    groups = channels // LANES
    received = passed_along(x_branch[length - width :], "seq", 1)
    leading_shard = lax.axis_index("seq") == 0
    tail = jnp.where(leading_shard, carry_tail, received)
    padded = jnp.concatenate([tail, x_branch], axis=0).astype(jnp.float32)
    convolved = conv_bias.astype(jnp.float32)
    for k in range(conv_weight.shape[0]):
        convolved = convolved + conv_weight[k].astype(jnp.float32) * padded[k : k + length]
    row_count = length * prompts
    activated = jax.nn.silu(convolved).reshape(row_count, channels)
    flat_act = activated.astype(jnp.bfloat16)
    projected = expert_sum(jnp.dot(flat_act, x_proj, preferred_element_type=jnp.float32))
    low_rank = dt_proj.shape[0]
    state_size = a_log.shape[1]
    low = projected[:, :low_rank].astype(jnp.bfloat16)
    bc = projected[:, low_rank:].reshape(-1)
    alog = a_log.T.reshape(state_size, groups, LANES)
    dtx, actx, state, total = local_states(
        low, dt_proj, dt_bias.reshape(1, channels), activated, alog, bc, prompts
    )
    sent = jnp.concatenate([total[:, None], state], axis=1)
    gathered = state_gather(sent)
    carry = carry_state.transpose(0, 2, 1).reshape(prompts, state_size, groups, LANES)
    entering = entering_state(gathered[:, :, 0], gathered[:, :, 1:], alog, carry)
    gated = gated_output(
        dtx, actx, alog, bc, entering, d_skip.reshape(groups, LANES), gate_branch.reshape(row_count, channels)
    )
    d_model = out_proj.shape[1]
    owner = lax.axis_index("expert")
    own_length = layer_input.shape[0]
    top_count = expert_ids.shape[-1]
    experts = router.shape[1]
    capacity = row_count * top_count * 5 // (4 * experts)
    capacity = (capacity + 15) // 16 * 16
    row_ids = expert_ids.reshape(row_count, top_count)
    slots = slot_matrix(row_ids, owner, capacity)
    slots16 = slots.astype(jnp.bfloat16)
    own_residual, normed = mix(
        gated,
        out_proj,
        layer_input.reshape(own_length * prompts, d_model),
        steering.reshape(1, d_model),
        refusal,
        norm_gain.reshape(1, d_model),
    )
    weight_rows = owner_weight(normed, router, row_ids, owner)
    expert_in = jnp.dot(slots16, normed, preferred_element_type=jnp.float32).astype(jnp.bfloat16)
    slot_weight = jnp.sum(jnp.where(slots, weight_rows[None, :], 0.0), axis=1)
    out = run_experts(
        expert_in,
        specialist_switch_matrix[0],
        w_up[0],
        w_down[0],
        slots16.T,
        slot_weight[:, None],
        own_residual,
    )
    return out.reshape(own_length, prompts, d_model)


def solution(mesh):
    return jax.shard_map(
        shards,
        mesh=mesh,
        in_specs=(
            P(("seq", "expert"), None, None),
            P("seq", None, "expert"),
            P("seq", None, "expert"),
            P(None, "expert"),
            P("expert"),
            P("expert", None),
            P(None, "expert"),
            P("expert"),
            P("expert", None),
            P("expert"),
            P(None, "expert", None),
            P(None, None, "expert"),
            P("expert", None),
            P(),
            P(),
            P(),
            P(),
            P("expert", None, "seq"),
            P("expert", None, "seq"),
            P("expert", "seq", None),
            P("seq", None, None),
        ),
        out_specs=P(("seq", "expert"), None, None),
        check_vma=False,
    )
```
